32 devices in a mesh: shot: 4 (over y, x), tx: 4 (over z), ty: 2 (over core).
Axes of the slice: x: 2, y: 2, z: 4, core: 2. Of those that a mesh axis runs over, the one named last changes fastest.
Arguments:
- forward_prev: float32 [4, 128, 16, 256], P('shot', 'tx', 'ty'), may hold values from -6 to 6
- forward_now: float32 [4, 128, 16, 256], P('shot', 'tx', 'ty'), may hold values from -6 to 6
- adjoint_prev: float32 [4, 128, 16, 256], P('shot', 'tx', 'ty'), may hold values from -6 to 6
- adjoint_now: float32 [4, 128, 16, 256], P('shot', 'tx', 'ty'), may hold values from -6 to 6
- velocity_model: bfloat16 [8, 128, 8, 256], P(('tx', 'ty'), 'shot'), may hold values from 1.5 to 4.5
- aperture: int32 [4, 8, 32], P('shot', ('tx', 'ty')), may hold values from 0 to 127, as said below
- source_cell: int32 [4, 2], P('shot'), may hold values from 0 to 127, as said below
- source_strength: float32 [4], P('shot'), may hold values from -60 to 60
- receiver_cell: int32 [4, 128, 2], P('shot'), may hold values from 0 to 127, as said below
- receiver_trace: float32 [4, 128], P('shot'), may hold values from -60 to 60
Outputs:
- forward_next: float32 [4, 128, 16, 256], P('shot', 'tx', 'ty')
- adjoint_next: float32 [4, 128, 16, 256], P('shot', 'tx', 'ty')
- image_slab: float32 [8, 128, 8, 256], P(('tx', 'ty'), 'shot')
The draws below stay inside these ranges and needn't reach their ends.
Inputs may be any that keep to these rules, and one draw needn't show every extreme that they name: `aperture`: each list of 32 block ids (one shot, one tile position) names every owner, id // 32, at most 8 times, and some owner exactly 8 times. `source_cell`: first entry below 128, second below 16. `receiver_cell`: first entry below 128, second below 16; receivers may share a cell.
All inputs are finite; a program needn't handle non-finite values.
Results may differ from the reference program's by a relative error of at most 0.0004.
Values may be sent and summed in bfloat16 or wider, within the bound.
No kernel may reach another device: no remote copies, remote signals or barrier semaphores. Data moves between devices by JAX's collectives and lax.ppermute only.
A program may use at most 64 MiB of HBM per device.

```python
import jax
import jax.numpy as jnp
from jax import lax

CX = 32
CY = 8
CZ = 256
SLAB = 32
NREC = 128
SURFACE_DEPTH = 8
CAP = 8
NTILE = 8
NBLK = 128
NX = 128
NY = 16
N_SHOT = 4
N_TX = 4
N_TY = 2


def draw_aperture(key, part):
    list_total = N_SHOT * NTILE
    row_keys = jax.random.split(key, list_total)
    marked_list = jax.random.randint(jax.random.fold_in(key, 11), (), 0, list_total)
    last_owner = N_SHOT - 1

    def one_list(row_key, list_number):
        key_owner, key_order, key_local = jax.random.split(row_key, 3)
        shuffled = jax.random.permutation(key_owner, N_SHOT).astype(jnp.int32)
        forced = list_number == marked_list
        spot = jnp.sum(jnp.where(shuffled == last_owner, jnp.arange(N_SHOT), 0))
        first_value = shuffled[0]
        swapped = jnp.where(jnp.arange(N_SHOT) == spot, first_value, shuffled)
        swapped = jnp.where(jnp.arange(N_SHOT) == 0, last_owner, swapped)
        shuffled = jnp.where(forced, swapped, shuffled)
        places = jnp.arange(CX)
        owner_slot = jnp.where(places < CAP, 0, 1 + (places - CAP) % max(N_SHOT - 1, 1))
        owners = shuffled[owner_slot]
        owners = owners[jax.random.permutation(key_order, CX)]
        local_ids = jax.random.randint(key_local, (CX,), 0, SLAB)
        local_ids = jnp.where(forced & (owners == last_owner), SLAB - 1, local_ids)
        return (owners * SLAB + local_ids).astype(jnp.int32)
    lists = jax.vmap(one_list)(row_keys, jnp.arange(list_total))
    return lists.reshape(N_SHOT, NTILE, CX)


def draw_source_cell(key, part):
    key_first, key_second, key_pick = jax.random.split(key, 3)
    along_x = jax.random.randint(key_first, (N_SHOT,), 0, NX)
    along_y = jax.random.randint(key_second, (N_SHOT,), 0, NY)
    picks = jax.random.randint(key_pick, (2,), 0, N_SHOT)
    shots = jnp.arange(N_SHOT)
    along_x = jnp.where(shots == picks[0], NX - 1, along_x)
    along_y = jnp.where(shots == picks[1], NY - 1, along_y)
    return jnp.stack([along_x, along_y], axis=1).astype(jnp.int32)


def draw_receiver_cell(key, part):
    key_first, key_second, key_pick = jax.random.split(jax.random.fold_in(key, 7), 3)
    along_x = jax.random.randint(key_first, (N_SHOT, NREC), 0, NX)
    along_y = jax.random.randint(key_second, (N_SHOT, NREC), 0, NY)
    picks = jax.random.randint(key_pick, (2,), 0, N_SHOT * NREC)
    flat = jnp.arange(N_SHOT * NREC).reshape(N_SHOT, NREC)
    along_x = jnp.where(flat == picks[0], NX - 1, along_x)
    along_y = jnp.where(flat == picks[1], NY - 1, along_y)
    return jnp.stack([along_x, along_y], axis=2).astype(jnp.int32)


def levels(rng, shape, cuts, low, largest):
    level, own = 1.0, jax.random.fold_in(rng, 6)
    for dim, parts in cuts:
        heights = jnp.exp(jax.random.uniform(jax.random.fold_in(own, dim), (parts,), jnp.float32, low / len(cuts), largest / len(cuts)))
        level = level * jnp.repeat(heights, shape[dim] // parts).reshape([-1 if axis == dim else 1 for axis in range(len(shape))])
    return level


def noise(stream_key, dims, spread, most, shards=(), kind=jnp.bfloat16):
    gain = levels(stream_key, dims, shards, -0.22, 0.18) if shards else 1.0
    result = jax.random.normal(stream_key, dims, jnp.float32) * spread * gain
    return jnp.minimum(jnp.maximum(result, -most), most).astype(kind)


def setup_inputs(seed: int = 0) -> dict:
    keys = jax.random.split(jax.random.key(seed), 11)
    return {
        "forward_prev": noise(keys[0], (N_SHOT, NX, NY, CZ), 1.0, 6.0, ((0, 4), (1, 4), (2, 2)), jnp.float32),
        "forward_now": noise(keys[1], (N_SHOT, NX, NY, CZ), 1.0, 6.0, ((0, 4), (1, 4), (2, 2)), jnp.float32),
        "adjoint_prev": noise(keys[2], (N_SHOT, NX, NY, CZ), 1.0, 6.0, ((0, 4), (1, 4), (2, 2)), jnp.float32),
        "adjoint_now": noise(keys[3], (N_SHOT, NX, NY, CZ), 1.0, 6.0, ((0, 4), (1, 4), (2, 2)), jnp.float32),
        "velocity_model": jnp.clip(1.5 + 3.0 * jax.random.uniform(keys[4], (NTILE, NBLK, CY, CZ), jnp.float32) ** levels(keys[4], (NTILE, NBLK, CY, CZ), ((0, 8), (1, 4)), -0.2, 0.2), 1.5, 4.5).astype(jnp.bfloat16),
        "aperture": draw_aperture(jax.random.fold_in(keys[10], 71), 0),
        "source_cell": draw_source_cell(jax.random.fold_in(keys[10], 71), 0),
        "source_strength": noise(keys[7], (N_SHOT,), 10.0, 60.0, ((0, 4),), jnp.float32),
        "receiver_cell": draw_receiver_cell(jax.random.fold_in(keys[10], 71), 0),
        "receiver_trace": noise(keys[9], (N_SHOT, NREC), 10.0, 60.0, ((0, 4),), jnp.float32),
    }


STENCIL_WEIGHTS = (-205.0 / 72.0, 8.0 / 5.0, -1.0 / 5.0, 8.0 / 315.0, -1.0 / 560.0)
STEP_RATIO = 0.1


def laplacian(padded):
    extent_x = padded.shape[-3] - 8
    extent_y = padded.shape[-2] - 8
    extent_z = padded.shape[-1] - 8
    centre = padded[..., 4:4 + extent_x, 4:4 + extent_y, 4:4 + extent_z]
    summed = (3.0 * STENCIL_WEIGHTS[0]) * centre
    for offset in range(1, 5):
        neighbours = (padded[..., 4 + offset:4 + offset + extent_x, 4:4 + extent_y, 4:4 + extent_z]
                      + padded[..., 4 - offset:4 - offset + extent_x, 4:4 + extent_y, 4:4 + extent_z]
                      + padded[..., 4:4 + extent_x, 4 + offset:4 + offset + extent_y, 4:4 + extent_z]
                      + padded[..., 4:4 + extent_x, 4 - offset:4 - offset + extent_y, 4:4 + extent_z]
                      + padded[..., 4:4 + extent_x, 4:4 + extent_y, 4 + offset:4 + offset + extent_z]
                      + padded[..., 4:4 + extent_x, 4:4 + extent_y, 4 - offset:4 - offset + extent_z])
        summed = summed + STENCIL_WEIGHTS[offset] * neighbours
    return summed


def injections(anchor_x, anchor_y, cells_x, cells_y, cells_z, source_xy, strength, receiver_xy, traces):
    grid_x = lax.iota(jnp.int32, cells_x) + anchor_x
    grid_y = lax.iota(jnp.int32, cells_y) + anchor_y
    depth_mark = (lax.iota(jnp.int32, cells_z) == SURFACE_DEPTH).astype(jnp.float32)
    mark_x = (grid_x == source_xy[0]).astype(jnp.float32)
    mark_y = (grid_y == source_xy[1]).astype(jnp.float32)
    injected = strength * mark_x[:, None, None] * mark_y[None, :, None] * depth_mark[None, None, :]
    receiver_x = (receiver_xy[:, 0][:, None] == grid_x[None, :]).astype(jnp.float32) * traces[:, None]
    receiver_y = (receiver_xy[:, 1][:, None] == grid_y[None, :]).astype(jnp.float32)
    surface = jnp.dot(receiver_x.T, receiver_y, precision=lax.Precision.HIGHEST)
    recorded = surface[:, :, None] * depth_mark[None, None, :]
    return injected, recorded


def reference(forward_prev, forward_now, adjoint_prev, adjoint_now, velocity_model, aperture,
              source_cell, source_strength, receiver_cell, receiver_trace):
    tile_index = jnp.arange(NTILE, dtype=jnp.int32)[:, None]

    def one_shot(image_sum, inputs):
        f_prev, f_now, a_prev, a_now, block_ids, source_xy, strength, receiver_xy, traces = inputs
        tiles = velocity_model[tile_index, block_ids].astype(jnp.float32)
        tiles = tiles.reshape(N_TX, N_TY, CX, CY, CZ).transpose(0, 2, 1, 3, 4).reshape(NX, NY, CZ)
        scaled = tiles * STEP_RATIO
        courant = scaled * scaled
        injected, recorded = injections(0, 0, NX, NY, CZ, source_xy, strength, receiver_xy, traces)
        pads = ((4, 4), (4, 4), (4, 4))
        f_next = 2.0 * f_now - f_prev + courant * (laplacian(jnp.pad(f_now, pads)) + injected)
        a_next = 2.0 * a_now - a_prev + courant * (laplacian(jnp.pad(a_now, pads)) + recorded)
        correlation = (f_next * a_next).reshape(N_TX, CX, N_TY, CY, CZ).transpose(0, 2, 1, 3, 4)
        correlation = correlation.reshape(NTILE, CX, CY, CZ)
        image_sum = image_sum.at[tile_index, block_ids].add(correlation)
        return image_sum, (f_next, a_next)

    start_image = jnp.zeros((NTILE, NBLK, CY, CZ), jnp.float32)
    image_slab, outputs = lax.scan(one_shot, start_image,
                                   (forward_prev, forward_now, adjoint_prev, adjoint_now, aperture,
                                    source_cell, source_strength, receiver_cell, receiver_trace))
    return outputs[0], outputs[1], image_slab
```

```python
import functools

import jax
import jax.numpy as jnp
from jax import lax
from jax.experimental import pallas as pl
from jax.experimental.pallas import tpu as pltpu
from jax.sharding import PartitionSpec as P

SURFACE_DEPTH = 8


STENCIL_WEIGHTS = (-205.0 / 72.0, 8.0 / 5.0, -1.0 / 5.0, 8.0 / 315.0, -1.0 / 560.0)
STEP_RATIO = 0.1
REACH = 4

VMEM = pl.BlockSpec(memory_space=pltpu.VMEM)
SMEM = pl.BlockSpec(memory_space=pltpu.SMEM)


def swaps(count):
    even = [(i, i + 1) for i in range(0, count - 1, 2)]
    odd = [(i, i + 1) for i in range(1, count - 1, 2)]
    return [[pair for a, b in pairs for pair in ((a, b), (b, a))] for pairs in (even, odd)]


def pack_kernel(where_ref, f_ref, a_ref, x_even_ref, x_odd_ref, y_even_ref, y_odd_ref=None):
    cells_x, cells_y, _ = f_ref.shape
    half = cells_x // 2
    x_at_even = where_ref[0] % 2 == 0
    y_at_even = where_ref[1] % 2 == 0
    tail, head = cells_x - REACH, 0
    start_even = jnp.where(x_at_even, tail, head)
    start_odd = jnp.where(x_at_even, head, tail)
    for field, ref in enumerate((f_ref, a_ref)):
        x_even_ref[field] = ref[pl.ds(start_even, REACH)]
        x_odd_ref[field] = ref[pl.ds(start_odd, REACH)]
        cells = ref[...]
        turned = jnp.roll(cells, REACH, axis=1)
        low = lax.broadcasted_iota(jnp.int32, (half,) + cells.shape[1:], 1) < REACH
        heads = jnp.where(low, cells[:half], turned[half:])
        tails = jnp.where(low, turned[:half], cells[half:])
        y_even_ref[field] = jnp.where(y_at_even, tails, heads)
        if y_odd_ref is not None:
            y_odd_ref[field] = jnp.where(y_at_even, heads, tails)


def stencil_kernel(count_y, where_ref, source_ref, strength_ref, cell_ref, trace_ref, f_ref, a_ref, *refs):
    if count_y > 2:
        x_even_ref, x_odd_ref, y_even_ref, y_odd_ref, out_ref, pad_ref, edge_ref = refs
    else:
        x_even_ref, x_odd_ref, y_even_ref, out_ref, pad_ref, edge_ref = refs
        y_odd_ref = None
    cells_x, cells_y, cells_z = f_ref.shape
    half = cells_x // 2
    x_at_even = where_ref[0] % 2 == 0
    y_at_even = where_ref[1] % 2 == 0
    row = lax.broadcasted_iota(jnp.int32, (cells_z, cells_z), 0)
    col = lax.broadcasted_iota(jnp.int32, (cells_z, cells_z), 1)
    gap = jnp.abs(row - col)
    band = jnp.zeros((cells_z, cells_z), jnp.float32)
    for offset in range(1, REACH + 1):
        band = jnp.where(gap == offset, STENCIL_WEIGHTS[offset], band)
    sub = lax.broadcasted_iota(jnp.int32, (cells_y, cells_z), 0)
    lane = lax.broadcasted_iota(jnp.int32, (cells_y, cells_z), 1)
    low = lax.broadcasted_iota(jnp.int32, (half, cells_y, cells_z), 1) < REACH

    cells = lax.broadcasted_iota(jnp.int32, (cells_x, cells_y, cell_ref.shape[1]), 0) * cells_y
    cells = cells + lax.broadcasted_iota(jnp.int32, cells.shape, 1)
    hit = jnp.where(cells == cell_ref[...][None], trace_ref[...][None], 0.0)
    surface = jnp.sum(hit, axis=2, keepdims=True)

    for field, ref in enumerate((f_ref, a_ref)):
        even, odd = x_even_ref[field], x_odd_ref[field]
        pad_ref[:REACH] = jnp.where(x_at_even, odd, even)
        pad_ref[REACH + cells_x :] = jnp.where(x_at_even, even, odd)
        cells = ref[...]
        pad_ref[REACH : REACH + cells_x] = cells
        even = y_even_ref[field]
        turned = jnp.roll(even, REACH, axis=1)
        if y_odd_ref is not None:
            odd = y_odd_ref[field]
            turned_odd = jnp.roll(odd, REACH, axis=1)
        else:
            odd = turned_odd = jnp.zeros_like(even)
        after_first = jnp.where(y_at_even, even, odd)
        after_second = jnp.where(y_at_even, turned, turned_odd)
        before_first = jnp.where(y_at_even, turned_odd, turned)
        before_second = jnp.where(y_at_even, odd, even)
        edge_ref[:half] = jnp.where(low, after_first, before_first)
        edge_ref[half:] = jnp.where(low, after_second, before_second)
        along_z = jnp.dot(
            cells.reshape(cells_x * cells_y, cells_z),
            band,
            precision=lax.Precision.HIGHEST,
            preferred_element_type=jnp.float32,
        )
        out_ref[field] = along_z.reshape(cells_x, cells_y, cells_z)

        def one_row(x, _, field=field):
            centre = pad_ref[x + REACH]
            edge = edge_ref[x]
            total = out_ref[field, x] + (3.0 * STENCIL_WEIGHTS[0]) * centre
            for offset in range(1, REACH + 1):
                after = jnp.roll(jnp.where(sub >= offset, centre, edge), -offset, axis=0)
                before = jnp.roll(jnp.where(sub < cells_y - offset, centre, edge), offset, axis=0)
                pairs = (pad_ref[x + REACH + offset] + pad_ref[x + REACH - offset]) + (after + before)
                total = total + STENCIL_WEIGHTS[offset] * pairs
            out_ref[field, x] = total
            return 0

        lax.fori_loop(0, cells_x, one_row, 0, unroll=4)
    depth = lax.broadcasted_iota(jnp.int32, (cells_x, cells_y, cells_z), 2) == SURFACE_DEPTH
    out_ref[1] = out_ref[1] + jnp.where(depth, surface, 0.0)
    source_x = source_ref[0] - where_ref[0] * cells_x
    source_y = source_ref[1] - where_ref[1] * cells_y

    @pl.when((source_x >= 0) & (source_x < cells_x))
    def _():
        mark = (sub == source_y) & (lane == SURFACE_DEPTH)
        out_ref[0, source_x] = out_ref[0, source_x] + jnp.where(mark, strength_ref[0], 0.0)


def rank_rows(ids_ref, rows_ref, taken_ref, owners, slab, capacity):
    for owner in range(owners):
        taken_ref[owner] = 0

    def one_row(r, _):
        owner = ids_ref[r] // slab
        slot = taken_ref[owner]
        rows_ref[owner * capacity + slot] = r
        taken_ref[owner] = slot + 1
        return 0

    lax.fori_loop(0, ids_ref.shape[0], one_row, 0, unroll=4)


def next_fields(r, block, v_ref, fields, curve_ref):
    f_prev_ref, f_now_ref, a_prev_ref, a_now_ref = fields
    scaled = v_ref[block] * STEP_RATIO
    courant = scaled * scaled
    f_next = 2.0 * f_now_ref[r] - f_prev_ref[r] + courant * curve_ref[0, r]
    a_next = 2.0 * a_now_ref[r] - a_prev_ref[r] + courant * curve_ref[1, r]
    return f_next, a_next


def send_kernel(owners, where_ref, ids_ref, *refs):
    fields, refs = refs[:4], refs[4:]
    curve_ref, refs = refs[0], refs[1:]
    slabs, refs = refs[: owners - 1], refs[owners - 1 :]
    outs, refs = refs[: owners - 1], refs[owners - 1 :]
    v_ref, rows_ref, taken_ref = refs
    slab = slabs[0].shape[0]
    capacity = outs[0].shape[0]
    rank_rows(ids_ref, rows_ref, taken_ref, owners, slab, capacity)
    me = where_ref[2]
    for k in range(1, owners):
        v_ref[...] = slabs[k - 1][...].astype(jnp.float32)
        for j in range(capacity):
            r = rows_ref[(me ^ k) * capacity + j]
            f_next, a_next = next_fields(r, ids_ref[r] % slab, v_ref, fields, curve_ref)
            outs[k - 1][j] = f_next * a_next


def output_kernel(owners, capacity, where_ref, *refs):
    lists, refs = refs[:owners], refs[owners:]
    fields, refs = refs[:4], refs[4:]
    curve_ref, refs = refs[0], refs[1:]
    slabs, refs = refs[:owners], refs[owners:]
    f_out_ref, a_out_ref, image_ref, places_ref, v_ref, rows_ref, taken_ref = refs
    ids_ref = lists[0]
    slab = slabs[0].shape[0]
    rank_rows(ids_ref, rows_ref, taken_ref, owners, slab, capacity)
    me = where_ref[2]
    image_ref[...] = jnp.zeros_like(image_ref)
    for k in range(owners):
        v_ref[...] = slabs[k][...].astype(jnp.float32)
        for j in range(capacity):
            r = rows_ref[(me ^ k) * capacity + j]
            block = ids_ref[r] % slab
            f_next, a_next = next_fields(r, block, v_ref, fields, curve_ref)
            f_out_ref[r] = f_next
            a_out_ref[r] = a_next
            if k == 0:
                image_ref[block] = image_ref[block] + f_next * a_next
    for k in range(1, owners):

        def one_row(r, slot, k=k):
            block = lists[k][r] - me * slab
            mine = (block >= 0) & (block < slab)

            @pl.when(mine)
            def _():
                places_ref[(k - 1) * capacity + slot] = block

            return slot + mine.astype(jnp.int32)

        lax.fori_loop(0, ids_ref.shape[0], one_row, 0)


def image_kernel(places_ref, own_ref, *refs):
    rows, out_ref = refs[:-1], refs[-1]
    capacity = rows[0].shape[0]
    out_ref[...] = own_ref[...]
    for k, ref in enumerate(rows):
        for j in range(capacity):
            block = places_ref[k * capacity + j]
            out_ref[block] = out_ref[block] + ref[j]


def on_device(
    forward_prev,
    forward_now,
    adjoint_prev,
    adjoint_now,
    velocity_model,
    aperture,
    source_cell,
    source_strength,
    receiver_cell,
    receiver_trace,
):
    owners = lax.axis_size("shot")
    count_x, count_y = lax.axis_size("tx"), lax.axis_size("ty")
    cells_x, cells_y, cells_z = forward_now.shape[1:]
    slab = velocity_model.shape[1]
    capacity = cells_x // owners
    fields = (forward_prev[0], forward_now[0], adjoint_prev[0], adjoint_now[0])
    at = [lax.axis_index("tx"), lax.axis_index("ty"), lax.axis_index("shot")]
    where = jnp.stack(at).astype(jnp.int32)
    ids = aperture[0, 0]

    def peer(value, k):
        return lax.ppermute(value, "shot", [(i, i ^ k) for i in range(owners)])

    slabs = [velocity_model[0]] + [peer(velocity_model[0], k) for k in range(1, owners)]
    lists = [ids] + [peer(ids, k) for k in range(1, owners)]

    f32 = jnp.float32
    x_face = jax.ShapeDtypeStruct((2, REACH, cells_y, cells_z), f32)
    y_face = jax.ShapeDtypeStruct((2, cells_x // 2, cells_y, cells_z), f32)
    faces = pl.pallas_call(
        pack_kernel,
        out_shape=(x_face, x_face, y_face) + ((y_face,) if count_y > 2 else ()),
        in_specs=[SMEM, VMEM, VMEM],
        out_specs=(VMEM,) * (4 if count_y > 2 else 3),
        name="pack_faces",
    )(where, fields[1], fields[3])
    x_even, x_odd = swaps(count_x)
    y_even, y_odd = swaps(count_y)
    halos = [lax.ppermute(faces[0], "tx", x_even), lax.ppermute(faces[1], "tx", x_odd)]
    halos.append(lax.ppermute(faces[2], "ty", y_even))
    if count_y > 2:
        halos.append(lax.ppermute(faces[3], "ty", y_odd))

    near_x = receiver_cell[0, :, 0] - at[0] * cells_x
    near_y = receiver_cell[0, :, 1] - at[1] * cells_y
    inside = (near_x >= 0) & (near_x < cells_x) & (near_y >= 0) & (near_y < cells_y)
    cell = jnp.where(inside, near_x * cells_y + near_y, -1)[None]

    curve = pl.pallas_call(
        functools.partial(stencil_kernel, count_y),
        out_shape=jax.ShapeDtypeStruct((2, cells_x, cells_y, cells_z), f32),
        in_specs=[SMEM, SMEM, SMEM, VMEM, VMEM, VMEM, VMEM] + [VMEM] * len(halos),
        out_specs=VMEM,
        scratch_shapes=[
            pltpu.VMEM((cells_x + 2 * REACH, cells_y, cells_z), f32),
            pltpu.VMEM((cells_x, cells_y, cells_z), f32),
        ],
        name="stencil",
    )(where, source_cell[0], source_strength, cell, receiver_trace, fields[1], fields[3], *halos)

    scratch = [
        pltpu.VMEM((slab, cells_y, cells_z), f32),
        pltpu.SMEM((cells_x,), jnp.int32),
        pltpu.SMEM((owners,), jnp.int32),
    ]
    row_block = jax.ShapeDtypeStruct((capacity, cells_y, cells_z), f32)
    to_send = pl.pallas_call(
        functools.partial(send_kernel, owners),
        out_shape=(row_block,) * (owners - 1),
        in_specs=[SMEM, SMEM] + [VMEM] * (5 + owners - 1),
        out_specs=(VMEM,) * (owners - 1),
        scratch_shapes=scratch,
        name="rows_to_send",
    )(where, ids, *fields, curve, *slabs[1:])
    arrived = [peer(rows, k) for k, rows in enumerate(to_send, 1)]

    field = jax.ShapeDtypeStruct((cells_x, cells_y, cells_z), f32)
    own = jax.ShapeDtypeStruct((slab, cells_y, cells_z), f32)
    table = jax.ShapeDtypeStruct(((owners - 1) * capacity,), jnp.int32)
    forward_next, adjoint_next, own_image, places = pl.pallas_call(
        functools.partial(output_kernel, owners, capacity),
        out_shape=(field, field, own, table),
        in_specs=[SMEM] * (1 + owners) + [VMEM] * (5 + owners),
        out_specs=(VMEM, VMEM, VMEM, SMEM),
        scratch_shapes=scratch,
        name="next_fields",
        cost_estimate=pl.CostEstimate(flops=2000000, bytes_accessed=3000000, transcendentals=0),
    )(where, *lists, *fields, curve, *slabs)

    image = pl.pallas_call(
        image_kernel,
        out_shape=own,
        in_specs=[SMEM] + [VMEM] * owners,
        out_specs=VMEM,
        name="image_rows",
    )(places, own_image, *arrived)
    return forward_next[None], adjoint_next[None], image[None]


def solution(mesh):
    in_specs = (
        P("shot", "tx", "ty", None),
        P("shot", "tx", "ty", None),
        P("shot", "tx", "ty", None),
        P("shot", "tx", "ty", None),
        P(("tx", "ty"), "shot", None, None),
        P("shot", ("tx", "ty"), None),
        P("shot", None),
        P("shot"),
        P("shot", None, None),
        P("shot", None),
    )
    out_specs = (
        P("shot", "tx", "ty", None),
        P("shot", "tx", "ty", None),
        P(("tx", "ty"), "shot", None, None),
    )
    return jax.shard_map(
        on_device, mesh=mesh, in_specs=in_specs, out_specs=out_specs, check_vma=False
    )
```

```python
import functools

import jax
import jax.numpy as jnp
from jax import lax
from jax.experimental import pallas as pl
from jax.experimental.pallas import tpu as pltpu
from jax.sharding import PartitionSpec as P

SURFACE_DEPTH = 8


STENCIL_WEIGHTS = (-205.0 / 72.0, 8.0 / 5.0, -1.0 / 5.0, 8.0 / 315.0, -1.0 / 560.0)
STEP_RATIO = 0.1
REACH = 4

VMEM = pl.BlockSpec(memory_space=pltpu.VMEM)
SMEM = pl.BlockSpec(memory_space=pltpu.SMEM)
PARAMS = pltpu.CompilerParams(vmem_limit_bytes=16 * 1024 * 1024)
F32, BF16 = jnp.float32, jnp.bfloat16


def swaps(count):
    even = [(i, i + 1) for i in range(0, count - 1, 2)]
    odd = [(i, i + 1) for i in range(1, count - 1, 2)]
    return [[pair for a, b in pairs for pair in ((a, b), (b, a))] for pairs in (even, odd)]


def halves(value):
    high = value.astype(BF16)
    return high, (value - high.astype(F32)).astype(BF16)


def product(left, right):
    (a, b), (c, d) = left, right

    def dot(x, y):
        return jnp.dot(x, y, preferred_element_type=F32)

    return dot(a, c) + (dot(a, d) + dot(b, c))


def by_distance(gap, stride=1):
    weights = jnp.zeros(gap.shape, F32)
    for offset in range(1, REACH + 1):
        weights = jnp.where(gap == offset * stride, STENCIL_WEIGHTS[offset], weights)
    return weights


def pack_kernel(f_ref, a_ref, x_even_ref, x_odd_ref, y_even_ref, y_odd_ref=None):
    cells_x, cells_y, cells_z = f_ref.shape
    half = cells_x // 2
    x_at_even = lax.axis_index("tx") % 2 == 0
    y_at_even = lax.axis_index("ty") % 2 == 0
    tail, head = cells_x - REACH, 0
    start_even = jnp.where(x_at_even, tail, head)
    start_odd = jnp.where(x_at_even, head, tail)
    low = (lax.broadcasted_iota(jnp.int32, (half, cells_y, cells_z), 1) < REACH).astype(jnp.int32)

    def face(ref, tails):
        turn = jnp.where(tails, 0, half)
        turned = pltpu.roll(ref[pl.ds(turn, half)], REACH, 1)
        straight = ref[pl.ds(half - turn, half)]
        return jnp.where(low == tails.astype(jnp.int32), turned, straight)

    for field, ref in enumerate((f_ref, a_ref)):
        x_even_ref[field] = ref[pl.ds(start_even, REACH)]
        x_odd_ref[field] = ref[pl.ds(start_odd, REACH)]
        y_even_ref[field] = face(ref, y_at_even)
        if y_odd_ref is not None:
            y_odd_ref[field] = face(ref, jnp.logical_not(y_at_even))


def inner_kernel(
    owners, slab, source_ref, strength_ref, receiver_ref, trace_ref, ids_ref, fp_ref, fn_ref, ap_ref, an_ref,
    out_ref, rows_ref, taken_ref,
):
    cells_x, cells_y, cells_z = fn_ref.shape
    cells = cells_x * cells_y
    capacity = cells_x // owners
    row = lax.broadcasted_iota(jnp.int32, (cells_z, cells_z), 0)
    col = lax.broadcasted_iota(jnp.int32, (cells_z, cells_z), 1)
    along_z = halves(by_distance(jnp.abs(row - col)))
    row = lax.broadcasted_iota(jnp.int32, (cells, cells), 0)
    col = lax.broadcasted_iota(jnp.int32, (cells, cells), 1)
    gap = jnp.abs(row - col)
    along_y = jnp.where(row // cells_y == col // cells_y, by_distance(gap), 0.0)
    along_xy = halves(along_y + by_distance(gap, cells_y))
    for field, (prev_ref, now_ref) in enumerate(((fp_ref, fn_ref), (ap_ref, an_ref))):
        now = now_ref[...].reshape(cells, cells_z)
        parts = halves(now)
        total = product(parts, along_z) + product(along_xy, parts)
        total = total + (3.0 * STENCIL_WEIGHTS[0]) * now
        out_ref[2 + field] = total.reshape(cells_x, cells_y, cells_z)
        out_ref[field] = 2.0 * now_ref[...] - prev_ref[...]

    start_x = lax.axis_index("tx") * cells_x
    start_y = lax.axis_index("ty") * cells_y
    near_x = receiver_ref[0:1, :] - start_x
    near_y = receiver_ref[1:2, :] - start_y
    cell_x = lax.broadcasted_iota(jnp.int32, (cells_x, cells_y, near_x.shape[1]), 0)
    cell_y = lax.broadcasted_iota(jnp.int32, cell_x.shape, 1)
    hit = jnp.where((cell_x == near_x[None]) & (cell_y == near_y[None]), trace_ref[...][None], 0.0)
    surface = jnp.sum(hit, axis=2, keepdims=True)
    lanes = min(cells_z, 128)
    depth = lax.broadcasted_iota(jnp.int32, (cells_x, cells_y, lanes), 2) == SURFACE_DEPTH
    out_ref[3, :, :, :lanes] = out_ref[3, :, :, :lanes] + jnp.where(depth, surface, 0.0)
    source_x = source_ref[0, 0] - start_x
    source_y = source_ref[0, 1] - start_y

    @pl.when((source_x >= 0) & (source_x < cells_x))
    def _():
        sub = lax.broadcasted_iota(jnp.int32, (cells_y, cells_z), 0)
        lane = lax.broadcasted_iota(jnp.int32, (cells_y, cells_z), 1)
        mark = (sub == source_y) & (lane == SURFACE_DEPTH)
        out_ref[2, source_x] = out_ref[2, source_x] + jnp.where(mark, strength_ref[0], 0.0)

    for owner in range(owners):
        taken_ref[owner] = 0

    def one_row(r, _):
        owner = ids_ref[0, 0, r] // slab
        slot = taken_ref[owner]
        rows_ref[owner * capacity + slot] = r
        taken_ref[owner] = slot + 1
        return 0

    lax.fori_loop(0, cells_x, one_row, 0, unroll=4)


def edge_kernel(x_even_ref, x_odd_ref, *refs):
    y_refs, (in_ref, out_ref) = refs[:-2], refs[-2:]
    _, cells_x, cells_y, cells_z = in_ref.shape
    half = cells_x // 2
    cells = cells_x * cells_y
    x_at_even = lax.axis_index("tx") % 2 == 0
    y_at_even = lax.axis_index("ty") % 2 == 0
    row = lax.broadcasted_iota(jnp.int32, (cells, half * cells_y), 0)
    col = lax.broadcasted_iota(jnp.int32, (cells, half * cells_y), 1)
    sub = col % cells_y
    same = row // cells_y == col // cells_y + half * (sub // REACH)
    layer, y = sub % REACH, row % cells_y
    after = by_distance(jnp.where(same, cells_y + layer - y, 0))
    before = by_distance(jnp.where(same, y + REACH - layer, 0))
    from_even = halves(jnp.where(y_at_even, after, before))
    from_odd = halves(jnp.where(y_at_even, before, after))
    for field in range(2):
        curve = in_ref[2 + field].reshape(cells, cells_z)
        for ref, weights in zip(y_refs, (from_even, from_odd)):
            curve = curve + product(weights, halves(ref[field].reshape(half * cells_y, cells_z)))
        out_ref[2 + field] = curve.reshape(cells_x, cells_y, cells_z)
        out_ref[field] = in_ref[field]
        before_x = jnp.where(x_at_even, x_odd_ref[field], x_even_ref[field])
        after_x = jnp.where(x_at_even, x_even_ref[field], x_odd_ref[field])
        for place in range(REACH):
            low = out_ref[2 + field, place]
            high = out_ref[2 + field, cells_x - REACH + place]
            for layer in range(REACH):
                if place + REACH - layer <= REACH:
                    low = low + STENCIL_WEIGHTS[place + REACH - layer] * before_x[layer]
                if layer + REACH - place <= REACH:
                    high = high + STENCIL_WEIGHTS[layer + REACH - place] * after_x[layer]
            out_ref[2 + field, place] = low
            out_ref[2 + field, cells_x - REACH + place] = high


def next_kernel(owners, rows_ref, ids_ref, *refs):
    state_ref, slabs, refs = refs[0], refs[1 : 1 + owners], refs[1 + owners :]
    messages, (f_out_ref, a_out_ref) = refs[:owners], refs[owners:]
    slab, cells_y, cells_z = slabs[0].shape
    capacity = f_out_ref.shape[0] // owners
    lanes = messages[0].shape[1]
    count = capacity * cells_y
    me = lax.axis_index("shot")
    lane = lax.broadcasted_iota(jnp.int32, (cells_y, lanes), 1) // cells_y
    for k in range(owners):
        place = jnp.zeros((cells_y, lanes), F32)
        for j in range(capacity):
            r = rows_ref[(me ^ k) * capacity + j]
            block = ids_ref[0, 0, r] % slab
            scaled = slabs[k][block].astype(F32) * STEP_RATIO
            courant = scaled * scaled
            f_next = state_ref[0, r] + courant * state_ref[2, r]
            a_next = state_ref[1, r] + courant * state_ref[3, r]
            f_out_ref[r] = f_next
            a_out_ref[r] = a_next
            image = f_next * a_next
            for part in range(cells_z // lanes):
                start = part * count + j * cells_y
                messages[k][start : start + cells_y, :] = image[:, part * lanes : (part + 1) * lanes]
            place = jnp.where(lane == j, block.astype(F32), place)
        messages[k][(cells_z // lanes) * count :, :] = place


def image_kernel(*refs):
    messages, out_ref = refs[:-1], refs[-1]
    slab, cells_y, cells_z = out_ref.shape
    lanes = messages[0].shape[1]
    parts = cells_z // lanes
    count = (messages[0].shape[0] - cells_y) // parts
    places = jnp.concatenate([ref[parts * count : parts * count + 1, :count] for ref in messages], axis=1)
    row = lax.broadcasted_iota(jnp.int32, (slab * cells_y, places.shape[1]), 0)
    col = lax.broadcasted_iota(jnp.int32, row.shape, 1)
    chosen = (row // cells_y == places.astype(jnp.int32)) & (row % cells_y == col % cells_y)
    chosen = jnp.where(chosen, 1.0, 0.0).astype(BF16)
    for part in range(parts):
        rows = jnp.concatenate([ref[part * count : (part + 1) * count, :] for ref in messages], axis=0)
        high, low = halves(rows)
        total = jnp.dot(chosen, high, preferred_element_type=F32) + jnp.dot(chosen, low, preferred_element_type=F32)
        out_ref[:, :, part * lanes : (part + 1) * lanes] = total.reshape(slab, cells_y, lanes)


def in_vmem(value):
    return pltpu.with_memory_space_constraint(value, pltpu.VMEM)


def in_smem(value):
    return pltpu.with_memory_space_constraint(value, pltpu.SMEM)


def on_device(
    forward_prev,
    forward_now,
    adjoint_prev,
    adjoint_now,
    velocity_model,
    aperture,
    source_cell,
    source_strength,
    receiver_cell,
    receiver_trace,
):
    owners = lax.axis_size("shot")
    count_x, count_y = lax.axis_size("tx"), lax.axis_size("ty")
    cells_x, cells_y, cells_z = forward_now.shape[1:]
    slab = velocity_model.shape[1]
    capacity = cells_x // owners
    forward_now, adjoint_now = in_vmem(forward_now[0]), in_vmem(adjoint_now[0])

    def peer(value, k):
        return lax.ppermute(value, "shot", [(i, i ^ k) for i in range(owners)])

    own_slab = velocity_model[0]
    slabs = [own_slab] + [peer(own_slab, k) for k in range(1, owners)]

    sides = 2 if count_y > 2 else 1
    x_face = pltpu.VMEM((2, REACH, cells_y, cells_z), F32)
    y_face = pltpu.VMEM((2, cells_x // 2, cells_y, cells_z), F32)
    faces = pl.pallas_call(
        pack_kernel,
        out_shape=(x_face, x_face) + (y_face,) * sides,
        in_specs=[VMEM, VMEM],
        out_specs=(VMEM,) * (2 + sides),
        compiler_params=PARAMS,
        name="pack_faces",
    )(forward_now, adjoint_now)
    halos = [lax.ppermute(face, "tx", pairs) for face, pairs in zip(faces[:2], swaps(count_x))]
    halos += [lax.ppermute(face, "ty", pairs) for face, pairs in zip(faces[2:], swaps(count_y))]

    state_shape = pltpu.VMEM((4, cells_x, cells_y, cells_z), F32)
    state, rows = pl.pallas_call(
        functools.partial(inner_kernel, owners, slab),
        out_shape=(state_shape, pltpu.SMEM((cells_x,), jnp.int32)),
        in_specs=[SMEM, SMEM, VMEM, VMEM, SMEM] + [VMEM] * 4,
        out_specs=(VMEM, SMEM),
        scratch_shapes=[pltpu.SMEM((owners,), jnp.int32)],
        compiler_params=PARAMS,
        name="inner_cells",
    )(
        source_cell,
        source_strength,
        receiver_cell[0].T,
        receiver_trace,
        aperture,
        in_vmem(forward_prev[0]),
        forward_now,
        in_vmem(adjoint_prev[0]),
        adjoint_now,
    )
    state = pl.pallas_call(
        edge_kernel,
        out_shape=state_shape,
        in_specs=[VMEM] * (len(halos) + 1),
        out_specs=VMEM,
        input_output_aliases={len(halos): 0},
        compiler_params=PARAMS,
        name="edge_cells",
    )(*[in_vmem(halo) for halo in halos], in_vmem(state))

    lanes = min(cells_z, 128)
    message = pltpu.VMEM(((cells_z // lanes) * capacity * cells_y + cells_y, lanes), F32)
    field = pltpu.VMEM((cells_x, cells_y, cells_z), F32)
    results = pl.pallas_call(
        functools.partial(next_kernel, owners),
        out_shape=(message,) * owners + (field, field),
        in_specs=[SMEM, SMEM] + [VMEM] * (1 + owners),
        out_specs=(VMEM,) * (owners + 2),
        compiler_params=PARAMS,
        name="next_cells",
    )(in_smem(rows), aperture, in_vmem(state), *[in_vmem(block) for block in slabs])
    messages, (forward_next, adjoint_next) = results[:owners], results[owners:]
    arrived = [messages[0]] + [peer(rows, k) for k, rows in enumerate(messages[1:], 1)]

    image = pl.pallas_call(
        image_kernel,
        out_shape=jax.ShapeDtypeStruct((slab, cells_y, cells_z), F32),
        in_specs=[VMEM] * owners,
        out_specs=VMEM,
        compiler_params=PARAMS,
        name="image_rows",
    )(*[in_vmem(rows) for rows in arrived])
    return forward_next[None], adjoint_next[None], image[None]


def solution(mesh):
    in_specs = (
        P("shot", "tx", "ty", None),
        P("shot", "tx", "ty", None),
        P("shot", "tx", "ty", None),
        P("shot", "tx", "ty", None),
        P(("tx", "ty"), "shot", None, None),
        P("shot", ("tx", "ty"), None),
        P("shot", None),
        P("shot"),
        P("shot", None, None),
        P("shot", None),
    )
    out_specs = (
        P("shot", "tx", "ty", None),
        P("shot", "tx", "ty", None),
        P(("tx", "ty"), "shot", None, None),
    )
    return jax.shard_map(
        on_device, mesh=mesh, in_specs=in_specs, out_specs=out_specs, check_vma=False
    )
```

```python
import functools

import jax
import jax.numpy as jnp
from jax import lax
from jax.experimental import pallas as pl
from jax.experimental.pallas import tpu as pltpu
from jax.sharding import PartitionSpec as P

SURFACE_DEPTH = 8


STENCIL_WEIGHTS = (-205.0 / 72.0, 8.0 / 5.0, -1.0 / 5.0, 8.0 / 315.0, -1.0 / 560.0)
STEP_RATIO = 0.1
REACH = 4

VMEM = pl.BlockSpec(memory_space=pltpu.VMEM)
SMEM = pl.BlockSpec(memory_space=pltpu.SMEM)
HBM = pl.BlockSpec(memory_space=pltpu.HBM)
CHEAP = pl.CostEstimate(flops=0, bytes_accessed=0, transcendentals=0)
PARAMS = pltpu.CompilerParams(vmem_limit_bytes=16 * 1024 * 1024)
F32, BF16 = jnp.float32, jnp.bfloat16


def swaps(axis, other):
    count, others = lax.axis_size(axis), lax.axis_size(other)
    even = [(i, i + 1) for i in range(0, count - 1, 2)]
    odd = [(i, i + 1) for i in range(1, count - 1, 2)]

    def rank(a, o):
        return a * others + o if axis == "tx" else o * count + a

    def ranks(pairs):
        return [(rank(a, o), rank(b, o)) for a, b in pairs for o in range(others)]

    idle = [i for i in range(count) if i not in {end for pair in odd for end in pair}]
    idle = [(rank(i, o), rank(i, o + 1)) for i in idle for o in range(0, others - 1, 2)]
    return [[way for a, b in pairs for way in ((a, b), (b, a))] for pairs in (ranks(even), ranks(odd) + idle)]


def has_odd(axis):
    at = lax.axis_index(axis)
    return jnp.where(at % 2 == 0, at > 0, at < lax.axis_size(axis) - 1)


def halves(value):
    high = value.astype(BF16)
    return high, (value - high.astype(F32)).astype(BF16)


def product(left, right):
    (a, b), (c, d) = left, right

    def dot(x, y):
        return jnp.dot(x, y, preferred_element_type=F32)

    return dot(a, c) + (dot(a, d) + dot(b, c))


def by_distance(gap, stride=1):
    weights = jnp.zeros(gap.shape, F32)
    for offset in range(1, REACH + 1):
        weights = jnp.where(gap == offset * stride, STENCIL_WEIGHTS[offset], weights)
    return weights


def load_kernel(f_hbm, a_hbm, v_hbm, f_ref, a_ref, v_ref, *refs):
    faces, sems = refs[:-1], refs[-1]
    sources, fields = (f_hbm, a_hbm, v_hbm), (f_ref, a_ref, v_ref)
    copies = [pltpu.make_async_copy(src, dst, sems.at[n]) for n, (src, dst) in enumerate(zip(sources, fields))]
    for copy in copies:
        copy.start()
    cells_x, cells_y, cells_z = f_ref.shape
    half = cells_x // 2
    at_even = lax.axis_index("ty") % 2 == 0
    low = (lax.broadcasted_iota(jnp.int32, (half, cells_y, cells_z), 1) < REACH).astype(jnp.int32)
    for field in range(2):
        ref = fields[field]
        copies[field].wait()
        for face, tails in zip(faces, (at_even, jnp.logical_not(at_even))):
            turn = jnp.where(tails, 0, half)
            turned = pltpu.roll(ref[pl.ds(turn, half)], REACH, 1)
            straight = ref[pl.ds(half - turn, half)]
            face[field] = jnp.where(low == tails.astype(jnp.int32), turned, straight)
    copies[2].wait()


def face_kernel(f_ref, a_ref, _, even_ref, odd_ref):
    at_even = lax.axis_index("tx") % 2 == 0
    tail, head = f_ref.shape[0] - REACH, 0
    for field, ref in enumerate((f_ref, a_ref)):
        even_ref[field] = ref[pl.ds(jnp.where(at_even, tail, head), REACH)]
        odd_ref[field] = ref[pl.ds(jnp.where(at_even, head, tail), REACH)]


def inner_kernel(
    owners, slab, strength_ref, source_hbm, receiver_hbm, trace_hbm, ids_hbm, fp_hbm, ap_hbm, fn_ref, an_ref,
    out_ref, rows_ref, blocks_ref, taken_ref, *scratch,
):
    cells_x, cells_y, cells_z = fn_ref.shape
    cells = cells_x * cells_y
    capacity = cells_x // owners
    scratch, sems = scratch[:-1], scratch[-1]
    source_ref, receiver_ref, trace_ref, ids_ref, fp_ref, ap_ref = scratch
    sources = (source_hbm, receiver_hbm, trace_hbm, ids_hbm, fp_hbm, ap_hbm)
    copies = [pltpu.make_async_copy(src, dst, sems.at[n]) for n, (src, dst) in enumerate(zip(sources, scratch))]
    for copy in copies:
        copy.start()
    row = lax.broadcasted_iota(jnp.int32, (cells_z, cells_z), 0)
    col = lax.broadcasted_iota(jnp.int32, (cells_z, cells_z), 1)
    along_z = halves(by_distance(jnp.abs(row - col)))
    row = lax.broadcasted_iota(jnp.int32, (cells, cells), 0)
    col = lax.broadcasted_iota(jnp.int32, (cells, cells), 1)
    gap = jnp.abs(row - col)
    along_y = jnp.where(row // cells_y == col // cells_y, by_distance(gap), 0.0)
    along_xy = halves(along_y + by_distance(gap, cells_y))
    for field, now_ref in enumerate((fn_ref, an_ref)):
        now = now_ref[...].reshape(cells, cells_z)
        parts = halves(now)
        total = product(parts, along_z) + product(along_xy, parts)
        total = total + (3.0 * STENCIL_WEIGHTS[0]) * now
        out_ref[2 + field] = total.reshape(cells_x, cells_y, cells_z)

    for copy in copies[:4]:
        copy.wait()
    start_x = lax.axis_index("tx") * cells_x
    start_y = lax.axis_index("ty") * cells_y
    near_x = receiver_ref[0:1, :] - start_x
    near_y = receiver_ref[1:2, :] - start_y
    cell_x = lax.broadcasted_iota(jnp.int32, (cells_x, cells_y, near_x.shape[1]), 0)
    cell_y = lax.broadcasted_iota(jnp.int32, cell_x.shape, 1)
    hit = jnp.where((cell_x == near_x[None]) & (cell_y == near_y[None]), trace_ref[...][None], 0.0)
    surface = jnp.sum(hit, axis=2, keepdims=True)
    lanes = min(cells_z, 128)
    depth = lax.broadcasted_iota(jnp.int32, (cells_x, cells_y, lanes), 2) == SURFACE_DEPTH
    out_ref[3, :, :, :lanes] = out_ref[3, :, :, :lanes] + jnp.where(depth, surface, 0.0)
    source_x = source_ref[0, 0] - start_x
    source_y = source_ref[0, 1] - start_y

    @pl.when((source_x >= 0) & (source_x < cells_x))
    def _():
        sub = lax.broadcasted_iota(jnp.int32, (cells_y, cells_z), 0)
        lane = lax.broadcasted_iota(jnp.int32, (cells_y, cells_z), 1)
        mark = (sub == source_y) & (lane == SURFACE_DEPTH)
        out_ref[2, source_x] = out_ref[2, source_x] + jnp.where(mark, strength_ref[0], 0.0)

    for owner in range(owners):
        taken_ref[owner] = 0

    def one_row(r, _):
        owner = ids_ref[0, 0, r] // slab
        slot = taken_ref[owner]
        rows_ref[owner * capacity + slot] = r
        blocks_ref[owner * capacity + slot] = ids_ref[0, 0, r] - owner * slab
        taken_ref[owner] = slot + 1
        return 0

    lax.fori_loop(0, cells_x, one_row, 0, unroll=4)
    for field, (copy, prev_ref, now_ref) in enumerate(zip(copies[4:], (fp_ref, ap_ref), (fn_ref, an_ref))):
        copy.wait()
        out_ref[field] = 2.0 * now_ref[...] - prev_ref[...]


def add_edges(state_ref, x_even_ref, x_odd_ref, y_refs, curve_ref):
    _, cells_x, cells_y, cells_z = curve_ref.shape
    half = cells_x // 2
    cells = cells_x * cells_y
    x_at_even = lax.axis_index("tx") % 2 == 0
    y_at_even = lax.axis_index("ty") % 2 == 0
    row = lax.broadcasted_iota(jnp.int32, (cells, half * cells_y), 0)
    col = lax.broadcasted_iota(jnp.int32, (cells, half * cells_y), 1)
    sub = col % cells_y
    same = row // cells_y == col // cells_y + half * (sub // REACH)
    layer, y = sub % REACH, row % cells_y
    after = by_distance(jnp.where(same, cells_y + layer - y, 0))
    before = by_distance(jnp.where(same, y + REACH - layer, 0))
    from_even = halves(jnp.where(y_at_even, after, before))
    from_odd = halves(jnp.where(has_odd("ty"), jnp.where(y_at_even, before, after), 0.0))
    x_has_odd = has_odd("tx")
    for field in range(2):
        curve = state_ref[2 + field].reshape(cells, cells_z)
        for ref, weights in zip(y_refs, (from_even, from_odd)):
            curve = curve + product(weights, halves(ref[field].reshape(half * cells_y, cells_z)))
        curve_ref[field] = curve.reshape(cells_x, cells_y, cells_z)
        x_odd = jnp.where(x_has_odd, x_odd_ref[field], 0.0)
        before_x = jnp.where(x_at_even, x_odd, x_even_ref[field])
        after_x = jnp.where(x_at_even, x_even_ref[field], x_odd)
        for place in range(REACH):
            low = curve_ref[field, place]
            high = curve_ref[field, cells_x - REACH + place]
            for layer in range(REACH):
                if place + REACH - layer <= REACH:
                    low = low + STENCIL_WEIGHTS[place + REACH - layer] * before_x[layer]
                if layer + REACH - place <= REACH:
                    high = high + STENCIL_WEIGHTS[layer + REACH - place] * after_x[layer]
            curve_ref[field, place] = low
            curve_ref[field, cells_x - REACH + place] = high


def courant_kernel(rows_ref, blocks_ref, *refs):
    slabs, out_ref = refs[:-1], refs[-1]
    capacity = out_ref.shape[0] // len(slabs)
    me = lax.axis_index("shot")
    for k, ref in enumerate(slabs):
        for j in range(capacity):
            slot = (me ^ k) * capacity + j
            scaled = ref[blocks_ref[slot]].astype(F32) * STEP_RATIO
            out_ref[rows_ref[slot]] = scaled * scaled


def scale_code(largest):
    least = jnp.maximum(largest, 2.0**-78) * (1.0 / 32752.0)
    exponent = jnp.floor(jnp.log2(least) + 1e-4)
    mantissa = jnp.ceil(least * jnp.exp2(7.0 - exponent))
    code = (exponent.astype(jnp.int32) + 30) * 512 + mantissa.astype(jnp.int32)
    return mantissa * jnp.exp2(exponent - 7.0), code


def scale_of(code):
    exponent = (code >> 9) - 37
    return (code & 511).astype(F32) * jnp.exp2(exponent.astype(F32))


def next_kernel(owners, rows_ref, blocks_ref, courant_ref, state_ref, x_even_ref, x_odd_ref, *refs):
    y_refs, refs = refs[: -owners - 3], refs[-owners - 3 :]
    messages, (f_out_ref, a_out_ref, curve_ref) = refs[:owners], refs[owners:]
    add_edges(state_ref, x_even_ref, x_odd_ref, y_refs, curve_ref)
    cells_x, cells_y, cells_z = f_out_ref.shape
    capacity = cells_x // owners
    lanes = messages[0].shape[1]
    parts = cells_z // lanes
    count = capacity * cells_y
    me = lax.axis_index("shot")
    lane = lax.broadcasted_iota(jnp.int32, (cells_y, lanes), 1) // cells_y
    for k in list(range(1, owners)) + [0]:
        place = jnp.zeros((cells_y, lanes), jnp.int32)
        images = []
        for j in range(capacity):
            slot = (me ^ k) * capacity + j
            r, block = rows_ref[slot], blocks_ref[slot]
            courant = courant_ref[r]
            f_next = state_ref[0, r] + courant * curve_ref[0, r]
            a_next = state_ref[1, r] + courant * curve_ref[1, r]
            f_out_ref[r] = f_next
            a_out_ref[r] = a_next
            images.append(f_next * a_next)
            place = jnp.where(lane == j, block, place)
        image = jnp.concatenate(images, axis=0)
        if k == 0:
            scales = jnp.ones((cells_y, lanes), jnp.int32)
        else:
            scale, code = scale_code(jnp.max(jnp.abs(image), axis=1, keepdims=True))
            image = jnp.round(image * (1.0 / scale)).astype(jnp.int32)
            scales = jnp.zeros((cells_y, lanes), jnp.int32)
            for j in range(capacity):
                scales = jnp.where(lane == j, code[j * cells_y : (j + 1) * cells_y], scales)
        kind = messages[k].dtype
        for part in range(parts):
            messages[k][part * count : (part + 1) * count, :] = image[:, part * lanes : (part + 1) * lanes].astype(kind)
        messages[k][parts * count :, :] = jnp.concatenate([scales, place], axis=0).astype(kind)


def image_kernel(*refs):
    messages, out_ref = refs[:-1], refs[-1]
    slab, cells_y, cells_z = out_ref.shape
    lanes = messages[0].shape[1]
    parts = cells_z // lanes
    count = (messages[0].shape[0] - 2 * cells_y) // parts
    scales, places = [], []
    for k, ref in enumerate(messages):
        tail = ref[parts * count :, :count].astype(jnp.int32)
        scale = scale_of(tail[:cells_y]) if k else jnp.ones((cells_y, count), F32)
        scales.append(scale)
        places.append(tail[cells_y:])
    scales, places = jnp.concatenate(scales, axis=1), jnp.concatenate(places, axis=1)
    shape = (slab,) + places.shape
    block = lax.broadcasted_iota(jnp.int32, shape, 0)
    y = lax.broadcasted_iota(jnp.int32, shape, 1)
    y_of_row = lax.broadcasted_iota(jnp.int32, shape, 2) % cells_y
    chosen = jnp.where((block == places[None]) & (y == y_of_row), scales[None], 0.0)
    chosen = chosen.reshape(slab * cells_y, places.shape[1]).astype(BF16)
    for part in range(parts):
        rows = [ref[part * count : (part + 1) * count, :].astype(F32) for ref in messages]
        high, low = halves(jnp.concatenate(rows, axis=0))
        total = jnp.dot(chosen, high, preferred_element_type=F32) + jnp.dot(chosen, low, preferred_element_type=F32)
        out_ref[:, :, part * lanes : (part + 1) * lanes] = total.reshape(slab, cells_y, lanes)


def in_vmem(value):
    return pltpu.with_memory_space_constraint(value, pltpu.VMEM)


def in_hbm(value):
    return pltpu.with_memory_space_constraint(value, pltpu.HBM)


def in_smem(value):
    return pltpu.with_memory_space_constraint(value, pltpu.SMEM)


def on_device(
    forward_prev,
    forward_now,
    adjoint_prev,
    adjoint_now,
    velocity_model,
    aperture,
    source_cell,
    source_strength,
    receiver_cell,
    receiver_trace,
):
    owners = lax.axis_size("shot")
    count_y = lax.axis_size("ty")
    cells_x, cells_y, cells_z = forward_now.shape[1:]
    slab = velocity_model.shape[1]
    capacity = cells_x // owners

    def peer(value, k):
        return lax.ppermute(value, "shot", [(i, i ^ k) for i in range(owners)])

    slabs = [peer(velocity_model[0], k) for k in range(1, owners)]

    sides = 2 if count_y > 2 else 1
    field = pltpu.VMEM((cells_x, cells_y, cells_z), F32)
    x_face = pltpu.VMEM((2, REACH, cells_y, cells_z), F32)
    y_face = pltpu.VMEM((2, cells_x // 2, cells_y, cells_z), F32)
    forward_now, adjoint_now, own_slab, *faces = pl.pallas_call(
        load_kernel,
        out_shape=(field, field, pltpu.VMEM(velocity_model.shape[1:], BF16)) + (y_face,) * sides,
        in_specs=[HBM] * 3,
        out_specs=(VMEM,) * (3 + sides),
        scratch_shapes=[pltpu.SemaphoreType.DMA((3,))],
        compiler_params=PARAMS,
        cost_estimate=CHEAP,
        name="load_fields",
    )(in_hbm(forward_now[0]), in_hbm(adjoint_now[0]), in_hbm(velocity_model[0]))
    forward_now, adjoint_now = in_vmem(forward_now), in_vmem(adjoint_now)
    slabs = [own_slab] + slabs
    halos = [in_vmem(lax.ppermute(face, ("tx", "ty"), pairs)) for face, pairs in zip(faces, swaps("ty", "tx"))]
    faces = pl.pallas_call(
        face_kernel,
        out_shape=(x_face, x_face),
        in_specs=[VMEM] * 3,
        out_specs=(VMEM, VMEM),
        compiler_params=PARAMS,
        cost_estimate=CHEAP,
        name="faces_along_x",
    )(forward_now, adjoint_now, halos[0])
    x_halos = [lax.ppermute(face, ("tx", "ty"), pairs) for face, pairs in zip(faces, swaps("tx", "ty"))]
    halos = [in_vmem(halo) for halo in x_halos] + halos

    table = pltpu.SMEM((cells_x,), jnp.int32)
    small = [source_cell, receiver_cell[0].T, receiver_trace, aperture]
    state, rows, blocks = pl.pallas_call(
        functools.partial(inner_kernel, owners, slab),
        out_shape=(pltpu.VMEM((4, cells_x, cells_y, cells_z), F32), table, table),
        in_specs=[SMEM] + [HBM] * 6 + [VMEM] * 2,
        out_specs=(VMEM, SMEM, SMEM),
        scratch_shapes=[
            pltpu.SMEM((owners,), jnp.int32),
            pltpu.SMEM(source_cell.shape, jnp.int32),
            pltpu.VMEM(small[1].shape, jnp.int32),
            pltpu.VMEM(receiver_trace.shape, F32),
            pltpu.SMEM(aperture.shape, jnp.int32),
            field,
            field,
            pltpu.SemaphoreType.DMA((6,)),
        ],
        compiler_params=PARAMS,
        cost_estimate=CHEAP,
        name="inner_cells",
    )(source_strength, *[in_hbm(value) for value in small + [forward_prev[0], adjoint_prev[0]]], forward_now, adjoint_now)
    rows, blocks = in_smem(rows), in_smem(blocks)
    courant = pl.pallas_call(
        courant_kernel,
        out_shape=field,
        in_specs=[SMEM] * 2 + [VMEM] * owners,
        out_specs=VMEM,
        compiler_params=PARAMS,
        cost_estimate=CHEAP,
        name="courant_rows",
    )(rows, blocks, *[in_vmem(block) for block in slabs])

    lanes = min(cells_z, 128)
    message = ((cells_z // lanes) * capacity * cells_y + 2 * cells_y, lanes)
    results = pl.pallas_call(
        functools.partial(next_kernel, owners),
        out_shape=(pltpu.VMEM(message, F32),) + (pltpu.VMEM(message, jnp.int16),) * (owners - 1) + (field, field),
        in_specs=[SMEM] * 2 + [VMEM] * (2 + len(halos)),
        out_specs=(VMEM,) * (owners + 2),
        scratch_shapes=[pltpu.VMEM((2, cells_x, cells_y, cells_z), F32)],
        compiler_params=PARAMS,
        name="next_cells",
    )(rows, blocks, in_vmem(courant), in_vmem(state), *halos)
    messages, (forward_next, adjoint_next) = results[:owners], results[owners:]
    arrived = [messages[0]] + [peer(rows, k) for k, rows in enumerate(messages[1:], 1)]

    image = pl.pallas_call(
        image_kernel,
        out_shape=jax.ShapeDtypeStruct((slab, cells_y, cells_z), F32),
        in_specs=[VMEM] * owners,
        out_specs=VMEM,
        compiler_params=PARAMS,
        name="image_rows",
    )(*[in_vmem(rows) for rows in arrived])
    return forward_next[None], adjoint_next[None], image[None]


def solution(mesh):
    in_specs = (
        P("shot", "tx", "ty", None),
        P("shot", "tx", "ty", None),
        P("shot", "tx", "ty", None),
        P("shot", "tx", "ty", None),
        P(("tx", "ty"), "shot", None, None),
        P("shot", ("tx", "ty"), None),
        P("shot", None),
        P("shot"),
        P("shot", None, None),
        P("shot", None),
    )
    out_specs = (
        P("shot", "tx", "ty", None),
        P("shot", "tx", "ty", None),
        P(("tx", "ty"), "shot", None, None),
    )
    return jax.shard_map(
        on_device, mesh=mesh, in_specs=in_specs, out_specs=out_specs, check_vma=False
    )
```

```python
import functools

import jax
import jax.numpy as jnp
from jax import lax
from jax.experimental import pallas as pl
from jax.experimental.pallas import tpu as pltpu
from jax.sharding import PartitionSpec as P

SURFACE_DEPTH = 8


STENCIL_WEIGHTS = (-205.0 / 72.0, 8.0 / 5.0, -1.0 / 5.0, 8.0 / 315.0, -1.0 / 560.0)
STEP_RATIO = 0.1
REACH = 4

VMEM = pl.BlockSpec(memory_space=pltpu.VMEM)
SMEM = pl.BlockSpec(memory_space=pltpu.SMEM)
HBM = pl.BlockSpec(memory_space=pltpu.HBM)
CHEAP = pl.CostEstimate(flops=0, bytes_accessed=0, transcendentals=0)
LONG = pl.CostEstimate(flops=0, bytes_accessed=60000000, transcendentals=0)
HEAVY = pl.CostEstimate(flops=10**10, bytes_accessed=10**8, transcendentals=10**8)
PARAMS = pltpu.CompilerParams(vmem_limit_bytes=16 * 1024 * 1024)
F32, BF16 = jnp.float32, jnp.bfloat16


def swaps(axis, other):
    count, others = lax.axis_size(axis), lax.axis_size(other)
    even = [(i, i + 1) for i in range(0, count - 1, 2)]
    odd = [(i, i + 1) for i in range(1, count - 1, 2)]

    def rank(a, o):
        return a * others + o if axis == "tx" else o * count + a

    def ranks(pairs):
        return [(rank(a, o), rank(b, o)) for a, b in pairs for o in range(others)]

    idle = [i for i in range(count) if i not in {end for pair in odd for end in pair}]
    idle = [(rank(i, o), rank(i, o + 1)) for i in idle for o in range(0, others - 1, 2)]
    return [[way for a, b in pairs for way in ((a, b), (b, a))] for pairs in (ranks(even), ranks(odd) + idle)]


def has_odd(axis):
    at = lax.axis_index(axis)
    return jnp.where(at % 2 == 0, at > 0, at < lax.axis_size(axis) - 1)


def halves(value):
    high = value.astype(BF16)
    return high, (value - high.astype(F32)).astype(BF16)


def product(left, right):
    (a, b), (c, d) = left, right

    def dot(x, y):
        return jnp.dot(x, y, preferred_element_type=F32)

    return dot(a, c) + (dot(a, d) + dot(b, c))


def by_distance(gap, stride=1):
    weights = jnp.zeros(gap.shape, F32)
    for offset in range(1, REACH + 1):
        weights = jnp.where(gap == offset * stride, STENCIL_WEIGHTS[offset], weights)
    return weights


def load_kernel(owners, slab, f_hbm, a_hbm, v_hbm, source_hbm, receiver_hbm, trace_hbm, ids_hbm, *refs):
    results, (ids_ref, taken_ref, sems) = refs[:-3], refs[-3:]
    f_ref, a_ref, v_ref, source_ref, receiver_ref, trace_ref, along_z_ref, along_xy_ref = results[:8]
    from_y_ref, rows_ref, blocks_ref = results[8:11]
    faces = results[11:]
    pairs = [(ids_hbm, ids_ref), (f_hbm, f_ref), (a_hbm, a_ref), (v_hbm, v_ref)]
    pairs += [(source_hbm, source_ref), (receiver_hbm, receiver_ref), (trace_hbm, trace_ref)]
    copies = [pltpu.make_async_copy(src, dst, sems.at[n]) for n, (src, dst) in enumerate(pairs)]
    for copy in copies:
        copy.start()
    cells_x, cells_y, cells_z = f_ref.shape
    cells = cells_x * cells_y
    capacity = cells_x // owners
    half = cells_x // 2
    row = lax.broadcasted_iota(jnp.int32, (cells_z, cells_z), 0)
    col = lax.broadcasted_iota(jnp.int32, (cells_z, cells_z), 1)
    along_z_ref[0], along_z_ref[1] = halves(by_distance(jnp.abs(row - col)))
    row = lax.broadcasted_iota(jnp.int32, (cells, cells), 0)
    col = lax.broadcasted_iota(jnp.int32, (cells, cells), 1)
    gap = jnp.abs(row - col)
    along_y = jnp.where(row // cells_y == col // cells_y, by_distance(gap), 0.0)
    along_xy_ref[0], along_xy_ref[1] = halves(along_y + by_distance(gap, cells_y))
    at_even = lax.axis_index("ty") % 2 == 0
    row = lax.broadcasted_iota(jnp.int32, (cells, half * cells_y), 0)
    col = lax.broadcasted_iota(jnp.int32, (cells, half * cells_y), 1)
    sub = col % cells_y
    same = row // cells_y == col // cells_y + half * (sub // REACH)
    layer, y = sub % REACH, row % cells_y
    after, before = cells_y + layer - y, y + REACH - layer
    from_y_ref[0], from_y_ref[1] = halves(by_distance(jnp.where(same, jnp.where(at_even, after, before), 0)))
    if len(faces) > 1:
        same &= has_odd("ty")
        from_y_ref[2], from_y_ref[3] = halves(by_distance(jnp.where(same, jnp.where(at_even, before, after), 0)))

    copies[0].wait()
    for owner in range(owners):
        taken_ref[owner] = 0

    def one_row(r, _):
        owner = ids_ref[0, 0, r] // slab
        slot = taken_ref[owner]
        rows_ref[owner * capacity + slot] = r
        blocks_ref[owner * capacity + slot] = ids_ref[0, 0, r] - owner * slab
        taken_ref[owner] = slot + 1
        return 0

    lax.fori_loop(0, cells_x, one_row, 0, unroll=4)
    low = (lax.broadcasted_iota(jnp.int32, (half, cells_y, cells_z), 1) < REACH).astype(jnp.int32)
    for field, ref in enumerate((f_ref, a_ref)):
        copies[1 + field].wait()
        for face, tails in zip(faces, (at_even, jnp.logical_not(at_even))):
            turn = jnp.where(tails, 0, half)
            turned = pltpu.roll(ref[pl.ds(turn, half)], REACH, 1)
            straight = ref[pl.ds(half - turn, half)]
            face[field] = jnp.where(low == tails.astype(jnp.int32), turned, straight).astype(BF16)
    for copy in copies[3:]:
        copy.wait()


def face_kernel(f_ref, a_ref, _, even_ref, odd_ref):
    at_even = lax.axis_index("tx") % 2 == 0
    tail, head = f_ref.shape[0] - REACH, 0
    for field, ref in enumerate((f_ref, a_ref)):
        even_ref[field] = ref[pl.ds(jnp.where(at_even, tail, head), REACH)].astype(BF16)
        odd_ref[field] = ref[pl.ds(jnp.where(at_even, head, tail), REACH)].astype(BF16)


def inner_kernel(
    strength_ref, source_ref, receiver_ref, trace_ref, along_z_ref, along_xy_ref, from_y_ref,
    fp_ref, ap_ref, fn_ref, an_ref, *refs,
):
    faces, out_ref = refs[:-1], refs[-1]
    cells_x, cells_y, cells_z = fn_ref.shape
    cells = cells_x * cells_y
    along_z = (along_z_ref[0], along_z_ref[1])
    along_xy = (along_xy_ref[0], along_xy_ref[1])
    for field, (prev_ref, now_ref) in enumerate(((fp_ref, fn_ref), (ap_ref, an_ref))):
        now = now_ref[...].reshape(cells, cells_z)
        parts = halves(now)
        total = product(parts, along_z) + product(along_xy, parts)
        total = total + (3.0 * STENCIL_WEIGHTS[0]) * now
        for side, ref in enumerate(faces):
            face = ref[field].astype(F32).reshape(cells // 2, cells_z).astype(BF16)
            for part in range(2):
                total = total + jnp.dot(from_y_ref[2 * side + part], face, preferred_element_type=F32)
        out_ref[2 + field] = total.reshape(cells_x, cells_y, cells_z)
        out_ref[field] = 2.0 * now_ref[...] - prev_ref[...]

    start_x = lax.axis_index("tx") * cells_x
    start_y = lax.axis_index("ty") * cells_y
    near_x = receiver_ref[0:1, :] - start_x
    near_y = receiver_ref[1:2, :] - start_y
    cell_x = lax.broadcasted_iota(jnp.int32, (cells_x, cells_y, near_x.shape[1]), 0)
    cell_y = lax.broadcasted_iota(jnp.int32, cell_x.shape, 1)
    hit = jnp.where((cell_x == near_x[None]) & (cell_y == near_y[None]), trace_ref[...][None], 0.0)
    surface = jnp.sum(hit, axis=2, keepdims=True)
    lanes = min(cells_z, 128)
    depth = lax.broadcasted_iota(jnp.int32, (cells_x, cells_y, lanes), 2) == SURFACE_DEPTH
    out_ref[3, :, :, :lanes] = out_ref[3, :, :, :lanes] + jnp.where(depth, surface, 0.0)
    source_x = source_ref[0, 0] - start_x
    source_y = source_ref[0, 1] - start_y

    @pl.when((source_x >= 0) & (source_x < cells_x))
    def _():
        sub = lax.broadcasted_iota(jnp.int32, (cells_y, cells_z), 0)
        lane = lax.broadcasted_iota(jnp.int32, (cells_y, cells_z), 1)
        mark = (sub == source_y) & (lane == SURFACE_DEPTH)
        out_ref[2, source_x] = out_ref[2, source_x] + jnp.where(mark, strength_ref[...], 0.0)


def edge_kernel(_, x_even_ref, x_odd_ref, state_ref):
    cells_x = state_ref.shape[1]
    at_even = lax.axis_index("tx") % 2 == 0
    for field in range(2):
        x_even = x_even_ref[field].astype(F32)
        x_odd = jnp.where(has_odd("tx"), x_odd_ref[field].astype(F32), 0.0)
        before_x = jnp.where(at_even, x_odd, x_even)
        after_x = jnp.where(at_even, x_even, x_odd)
        for place in range(REACH):
            low = state_ref[2 + field, place]
            high = state_ref[2 + field, cells_x - REACH + place]
            for layer in range(REACH):
                if place + REACH - layer <= REACH:
                    low = low + STENCIL_WEIGHTS[place + REACH - layer] * before_x[layer]
                if layer + REACH - place <= REACH:
                    high = high + STENCIL_WEIGHTS[layer + REACH - place] * after_x[layer]
            state_ref[2 + field, place] = low
            state_ref[2 + field, cells_x - REACH + place] = high


def scale_code(largest):
    least = jnp.maximum(largest, 2.0**-78) * (1.0 / 32752.0)
    exponent = jnp.floor(jnp.log2(least) + 1e-4)
    mantissa = jnp.ceil(least * jnp.exp2(7.0 - exponent))
    code = (exponent.astype(jnp.int32) + 30) * 512 + mantissa.astype(jnp.int32)
    return mantissa * jnp.exp2(exponent - 7.0), code


def scale_of(code):
    exponent = (code >> 9) - 37
    return (code & 511).astype(F32) * jnp.exp2(exponent.astype(F32))


def next_row(slot, rows_ref, blocks_ref, state_ref, slab_ref):
    r, block = rows_ref[slot], blocks_ref[slot]
    scaled = slab_ref[block].astype(F32) * STEP_RATIO
    courant = scaled * scaled
    f_next = state_ref[0, r] + courant * state_ref[2, r]
    a_next = state_ref[1, r] + courant * state_ref[3, r]
    return r, block, f_next, a_next


def send_kernel(k, rows_ref, blocks_ref, state_ref, slab_ref, message_ref, f_ref, a_ref):
    capacity, cells_y, cells_z = f_ref.shape
    lanes = message_ref.shape[1]
    parts = cells_z // lanes
    count = capacity * cells_y
    owner = lax.axis_index("shot") ^ k
    lane = lax.broadcasted_iota(jnp.int32, (cells_y, lanes), 1) // cells_y
    place = jnp.zeros((cells_y, lanes), jnp.int32)
    scales = jnp.zeros((cells_y, lanes), jnp.int32)
    images = []
    for j in range(capacity):
        _, block, f_next, a_next = next_row(owner * capacity + j, rows_ref, blocks_ref, state_ref, slab_ref)
        f_ref[j] = f_next
        a_ref[j] = a_next
        images.append(f_next * a_next)
        place = jnp.where(lane == j, block, place)
    image = jnp.concatenate(images, axis=0)
    scale, code = scale_code(jnp.max(jnp.abs(image), axis=1, keepdims=True))
    image = jnp.round(image * (1.0 / scale)).astype(jnp.int32)
    for j in range(capacity):
        scales = jnp.where(lane == j, code[j * cells_y : (j + 1) * cells_y], scales)
    for part in range(parts):
        columns = image[:, part * lanes : (part + 1) * lanes]
        message_ref[part * count : (part + 1) * count, :] = columns.astype(jnp.int16)
    message_ref[parts * count :, :] = jnp.concatenate([scales, place], axis=0).astype(jnp.int16)


def output_kernel(owners, rows_ref, blocks_ref, state_ref, slab_ref, *refs):
    others, (f_out_ref, a_out_ref, image_ref, place_ref) = refs[:-4], refs[-4:]
    cells_x, cells_y, cells_z = f_out_ref.shape
    capacity = cells_x // owners
    me = lax.axis_index("shot")
    lane = lax.broadcasted_iota(jnp.int32, place_ref.shape, 1) // cells_y
    place = jnp.zeros(place_ref.shape, jnp.int32)
    for j in range(capacity):
        r, block, f_next, a_next = next_row(me * capacity + j, rows_ref, blocks_ref, state_ref, slab_ref)
        f_out_ref[r] = f_next
        a_out_ref[r] = a_next
        image_ref[j] = f_next * a_next
        place = jnp.where(lane == j, block, place)
    place_ref[...] = place
    for n, k in enumerate(range(1, owners)):
        for j in range(capacity):
            r = rows_ref[(me ^ k) * capacity + j]
            f_out_ref[r] = others[2 * n][j]
            a_out_ref[r] = others[2 * n + 1][j]


def image_kernel(own_ref, own_place_ref, *refs):
    messages, (out_hbm, out_ref, sems) = refs[:-3], refs[-3:]
    slab, cells_y, cells_z = out_ref.shape
    lanes = messages[0].shape[1]
    parts = cells_z // lanes
    count = own_ref.shape[0] * cells_y
    scales, places = [jnp.ones((cells_y, count), F32)], [own_place_ref[:, :count]]
    for ref in messages:
        tail = ref[parts * count :, :count].astype(jnp.int32)
        scales.append(scale_of(tail[:cells_y]))
        places.append(tail[cells_y:])
    scales, places = jnp.concatenate(scales, axis=1), jnp.concatenate(places, axis=1)
    shape = (slab,) + places.shape
    block = lax.broadcasted_iota(jnp.int32, shape, 0)
    y = lax.broadcasted_iota(jnp.int32, shape, 1)
    y_of_row = lax.broadcasted_iota(jnp.int32, shape, 2) % cells_y
    chosen = jnp.where((block == places[None]) & (y == y_of_row), scales[None], 0.0)
    chosen = chosen.reshape(slab * cells_y, places.shape[1]).astype(BF16)
    rows = [own_ref[...].reshape(count, cells_z)]
    for ref in messages:
        columns = [ref[part * count : (part + 1) * count, :] for part in range(parts)]
        rows.append(jnp.concatenate(columns, axis=1).astype(F32))
    high, low = halves(jnp.concatenate(rows, axis=0))
    half = slab // 2
    copies = []
    for n in range(2):
        some = chosen[n * half * cells_y : (n + 1) * half * cells_y]
        total = jnp.dot(some, high, preferred_element_type=F32) + jnp.dot(some, low, preferred_element_type=F32)
        blocks = pl.ds(n * half, half)
        out_ref[blocks] = total.reshape(half, cells_y, cells_z)
        copies.append(pltpu.make_async_copy(out_ref.at[blocks], out_hbm.at[blocks], sems.at[n]))
        copies[n].start()
    for copy in copies:
        copy.wait()


def in_vmem(value):
    return pltpu.with_memory_space_constraint(value, pltpu.VMEM)


def in_hbm(value):
    return pltpu.with_memory_space_constraint(value, pltpu.HBM)


def in_smem(value):
    return pltpu.with_memory_space_constraint(value, pltpu.SMEM)


def on_device(
    forward_prev,
    forward_now,
    adjoint_prev,
    adjoint_now,
    velocity_model,
    aperture,
    source_cell,
    source_strength,
    receiver_cell,
    receiver_trace,
):
    owners = lax.axis_size("shot")
    count_y = lax.axis_size("ty")
    cells_x, cells_y, cells_z = forward_now.shape[1:]
    slab = velocity_model.shape[1]
    capacity = cells_x // owners

    def peer(value, k):
        return lax.ppermute(value, "shot", [(i, i ^ k) for i in range(owners)])

    others = list(range(1, owners))
    slabs = {k: peer(velocity_model[0], k) for k in others}

    sides = 2 if count_y > 2 else 1
    field = pltpu.VMEM((cells_x, cells_y, cells_z), F32)
    x_face = pltpu.VMEM((2, REACH, cells_y, cells_z), BF16)
    y_face = pltpu.VMEM((2, cells_x // 2, cells_y, cells_z), BF16)
    table = pltpu.SMEM((cells_x,), jnp.int32)
    sources = [forward_now[0], adjoint_now[0], velocity_model[0]]
    sources += [source_cell, receiver_cell[0].T, receiver_trace, aperture]
    forward_now, adjoint_now, own_slab, source, receiver, trace, along_z, along_xy, from_y, rows, blocks, *faces = (
        pl.pallas_call(
        functools.partial(load_kernel, owners, slab),
        out_shape=(
            field,
            field,
            pltpu.VMEM(velocity_model.shape[1:], BF16),
            pltpu.SMEM(source_cell.shape, jnp.int32),
            pltpu.VMEM(sources[4].shape, jnp.int32),
            pltpu.VMEM(receiver_trace.shape, F32),
            pltpu.VMEM((2, cells_z, cells_z), BF16),
            pltpu.VMEM((2, cells_x * cells_y, cells_x * cells_y), BF16),
            pltpu.VMEM((2 * sides, cells_x * cells_y, cells_x // 2 * cells_y), BF16),
            table,
            table,
        )
        + (y_face,) * sides,
        in_specs=[HBM] * 7,
        out_specs=(VMEM,) * 3 + (SMEM,) + (VMEM,) * 5 + (SMEM,) * 2 + (VMEM,) * sides,
        scratch_shapes=[
            pltpu.SMEM(aperture.shape, jnp.int32),
            pltpu.SMEM((owners,), jnp.int32),
            pltpu.SemaphoreType.DMA((7,)),
        ],
        compiler_params=PARAMS,
        cost_estimate=CHEAP,
        name="load_fields",
    )(*[in_hbm(value) for value in sources])
    )
    forward_now, adjoint_now = in_vmem(forward_now), in_vmem(adjoint_now)
    rows, blocks = in_smem(rows), in_smem(blocks)
    slabs[0] = own_slab
    y_halos = [in_vmem(lax.ppermute(face, ("tx", "ty"), pairs)) for face, pairs in zip(faces, swaps("ty", "tx"))]
    faces = pl.pallas_call(
        face_kernel,
        out_shape=(x_face, x_face),
        in_specs=[VMEM] * 3,
        out_specs=(VMEM, VMEM),
        compiler_params=PARAMS,
        cost_estimate=CHEAP,
        name="faces_along_x",
    )(forward_now, adjoint_now, y_halos[0])
    x_even, x_odd = swaps("tx", "ty")
    from_odd = lax.ppermute(faces[1], ("tx", "ty"), x_odd)
    from_even = lax.ppermute(faces[0], ("tx", "ty"), x_even)

    state = pl.pallas_call(
        inner_kernel,
        out_shape=pltpu.VMEM((4, cells_x, cells_y, cells_z), F32),
        in_specs=[VMEM, SMEM] + [VMEM] * (9 + sides),
        out_specs=VMEM,
        compiler_params=PARAMS,
        cost_estimate=LONG,
        name="inner_cells",
    )(
        source_strength[None],
        in_smem(source),
        in_vmem(receiver),
        in_vmem(trace),
        in_vmem(along_z),
        in_vmem(along_xy),
        in_vmem(from_y),
        forward_prev[0],
        adjoint_prev[0],
        forward_now,
        adjoint_now,
        *y_halos,
    )
    state = in_vmem(
        pl.pallas_call(
            edge_kernel,
            out_shape=pltpu.VMEM(state.shape, F32),
            in_specs=[VMEM] * 3,
            out_specs=VMEM,
            input_output_aliases={0: 0},
            compiler_params=PARAMS,
            cost_estimate=CHEAP,
            name="edge_cells",
        )(in_vmem(state), in_vmem(from_even), in_vmem(from_odd))
    )

    lanes = min(cells_z, 128)
    message = pltpu.VMEM(((cells_z // lanes) * capacity * cells_y + 2 * cells_y, lanes), jnp.int16)
    some_rows = pltpu.VMEM((capacity, cells_y, cells_z), F32)
    arrived, rows_of_others = [], []
    for k in others:
        rows_out, *fields = pl.pallas_call(
            functools.partial(send_kernel, k),
            out_shape=(message, some_rows, some_rows),
            in_specs=[SMEM] * 2 + [VMEM] * 2,
            out_specs=(VMEM,) * 3,
            compiler_params=PARAMS,
            cost_estimate=HEAVY if k == others[-2] else CHEAP,
            name="rows_to_send",
        )(rows, blocks, state, in_vmem(slabs[k]))
        arrived.append(peer(rows_out, k))
        rows_of_others += fields

    whole = jax.ShapeDtypeStruct((cells_x, cells_y, cells_z), F32)
    forward_next, adjoint_next, own_image, own_place = pl.pallas_call(
        functools.partial(output_kernel, owners),
        out_shape=(whole, whole, some_rows, pltpu.VMEM((cells_y, lanes), jnp.int32)),
        in_specs=[SMEM] * 2 + [VMEM] * (2 + len(rows_of_others)),
        out_specs=(VMEM,) * 4,
        compiler_params=PARAMS,
        cost_estimate=LONG,
        name="next_fields",
    )(rows, blocks, state, in_vmem(slabs[0]), *[in_vmem(other) for other in rows_of_others])

    image = pl.pallas_call(
        image_kernel,
        out_shape=jax.ShapeDtypeStruct((slab, cells_y, cells_z), F32),
        in_specs=[VMEM] * (1 + owners),
        out_specs=HBM,
        scratch_shapes=[pltpu.VMEM((slab, cells_y, cells_z), F32), pltpu.SemaphoreType.DMA((2,))],
        compiler_params=PARAMS,
        name="image_rows",
    )(in_vmem(own_image), in_vmem(own_place), *[in_vmem(value) for value in arrived])
    return forward_next[None], adjoint_next[None], image[None]


def solution(mesh):
    in_specs = (
        P("shot", "tx", "ty", None),
        P("shot", "tx", "ty", None),
        P("shot", "tx", "ty", None),
        P("shot", "tx", "ty", None),
        P(("tx", "ty"), "shot", None, None),
        P("shot", ("tx", "ty"), None),
        P("shot", None),
        P("shot"),
        P("shot", None, None),
        P("shot", None),
    )
    out_specs = (
        P("shot", "tx", "ty", None),
        P("shot", "tx", "ty", None),
        P(("tx", "ty"), "shot", None, None),
    )
    return jax.shard_map(
        on_device, mesh=mesh, in_specs=in_specs, out_specs=out_specs, check_vma=False
    )
```

```python
import functools

import jax
import jax.numpy as jnp
from jax import lax
from jax.experimental import pallas as pl
from jax.experimental.pallas import tpu as pltpu
from jax.sharding import PartitionSpec as P

SURFACE_DEPTH = 8


STENCIL_WEIGHTS = (-205.0 / 72.0, 8.0 / 5.0, -1.0 / 5.0, 8.0 / 315.0, -1.0 / 560.0)
STEP_RATIO = 0.1
REACH = 4

VMEM = pl.BlockSpec(memory_space=pltpu.VMEM)
SMEM = pl.BlockSpec(memory_space=pltpu.SMEM)
HBM = pl.BlockSpec(memory_space=pltpu.HBM)
CHEAP = pl.CostEstimate(flops=0, bytes_accessed=0, transcendentals=0)
LONG = pl.CostEstimate(flops=0, bytes_accessed=60000000, transcendentals=0)
HEAVY = pl.CostEstimate(flops=10**10, bytes_accessed=10**8, transcendentals=10**8)
PARAMS = pltpu.CompilerParams(vmem_limit_bytes=16 * 1024 * 1024)
F32, BF16 = jnp.float32, jnp.bfloat16


def swaps(axis, other):
    count, others = lax.axis_size(axis), lax.axis_size(other)
    even = [(i, i + 1) for i in range(0, count - 1, 2)]
    odd = [(i, i + 1) for i in range(1, count - 1, 2)]

    def rank(a, o):
        return a * others + o if axis == "tx" else o * count + a

    def ranks(pairs):
        return [(rank(a, o), rank(b, o)) for a, b in pairs for o in range(others)]

    idle = [i for i in range(count) if i not in {end for pair in odd for end in pair}]
    idle = [(rank(i, o), rank(i, o + 1)) for i in idle for o in range(0, others - 1, 2)]
    return [[way for a, b in pairs for way in ((a, b), (b, a))] for pairs in (ranks(even), ranks(odd) + idle)]


def has_odd(axis):
    at = lax.axis_index(axis)
    return jnp.where(at % 2 == 0, at > 0, at < lax.axis_size(axis) - 1)


def halves(value):
    high = value.astype(BF16)
    return high, (value - high.astype(F32)).astype(BF16)


def product(left, right):
    (a, b), (c, d) = left, right

    def dot(x, y):
        return jnp.dot(x, y, preferred_element_type=F32)

    return dot(a, c) + (dot(a, d) + dot(b, c))


def by_distance(gap, stride=1):
    weights = jnp.zeros(gap.shape, F32)
    for offset in range(1, REACH + 1):
        weights = jnp.where(gap == offset * stride, STENCIL_WEIGHTS[offset], weights)
    return weights


def load_kernel(owners, slab, f_hbm, a_hbm, v_hbm, source_hbm, receiver_hbm, trace_hbm, ids_hbm, *refs):
    results, (ids_ref, sems) = refs[:-2], refs[-2:]
    f_ref, a_ref, v_ref, source_ref, receiver_ref, trace_ref, along_z_ref, along_xy_ref = results[:8]
    from_y_ref, rows_ref, blocks_ref = results[8:11]
    faces = results[11:]
    pairs = [(ids_hbm, ids_ref), (f_hbm, f_ref), (a_hbm, a_ref), (v_hbm, v_ref)]
    pairs += [(source_hbm, source_ref), (receiver_hbm, receiver_ref), (trace_hbm, trace_ref)]
    copies = [pltpu.make_async_copy(src, dst, sems.at[n]) for n, (src, dst) in enumerate(pairs)]
    for copy in copies:
        copy.start()
    cells_x, cells_y, cells_z = f_ref.shape
    cells = cells_x * cells_y
    capacity = cells_x // owners
    half = cells_x // 2
    row = lax.broadcasted_iota(jnp.int32, (cells_z, cells_z), 0)
    col = lax.broadcasted_iota(jnp.int32, (cells_z, cells_z), 1)
    along_z_ref[0], along_z_ref[1] = halves(by_distance(jnp.abs(row - col)))
    row = lax.broadcasted_iota(jnp.int32, (cells, cells), 0)
    col = lax.broadcasted_iota(jnp.int32, (cells, cells), 1)
    gap = jnp.abs(row - col)
    along_y = jnp.where(row // cells_y == col // cells_y, by_distance(gap), 0.0)
    along_xy_ref[0], along_xy_ref[1] = halves(along_y + by_distance(gap, cells_y))
    at_even = lax.axis_index("ty") % 2 == 0
    row = lax.broadcasted_iota(jnp.int32, (cells, half * cells_y), 0)
    col = lax.broadcasted_iota(jnp.int32, (cells, half * cells_y), 1)
    sub = col % cells_y
    same = row // cells_y == col // cells_y + half * (sub // REACH)
    layer, y = sub % REACH, row % cells_y
    after, before = cells_y + layer - y, y + REACH - layer
    from_y_ref[0], from_y_ref[1] = halves(by_distance(jnp.where(same, jnp.where(at_even, after, before), 0)))
    if len(faces) > 1:
        same &= has_odd("ty")
        from_y_ref[2], from_y_ref[3] = halves(by_distance(jnp.where(same, jnp.where(at_even, before, after), 0)))

    copies[0].wait()
    bits = 32 // owners
    taken = jnp.int32(0)
    for r in range(cells_x):
        block = ids_ref[0, 0, r]
        owner = block // slab
        slot = owner * capacity + ((taken >> (owner * bits)) & (2**bits - 1))
        rows_ref[slot] = r
        blocks_ref[slot] = block - owner * slab
        taken = taken + (1 << (owner * bits))
    low = (lax.broadcasted_iota(jnp.int32, (half, cells_y, cells_z), 1) < REACH).astype(jnp.int32)
    for field, ref in enumerate((f_ref, a_ref)):
        copies[1 + field].wait()
        for face, tails in zip(faces, (at_even, jnp.logical_not(at_even))):
            turn = jnp.where(tails, 0, half)
            turned = pltpu.roll(ref[pl.ds(turn, half)], REACH, 1)
            straight = ref[pl.ds(half - turn, half)]
            face[field] = jnp.where(low == tails.astype(jnp.int32), turned, straight).astype(BF16)
    for copy in copies[3:]:
        copy.wait()


def after_kernel(in_ref, _, out_ref):
    out_ref[...] = in_ref[...]


def face_kernel(f_ref, a_ref, even_ref, odd_ref):
    at_even = lax.axis_index("tx") % 2 == 0
    tail, head = f_ref.shape[0] - REACH, 0
    for field, ref in enumerate((f_ref, a_ref)):
        even_ref[field] = ref[pl.ds(jnp.where(at_even, tail, head), REACH)].astype(BF16)
        odd_ref[field] = ref[pl.ds(jnp.where(at_even, head, tail), REACH)].astype(BF16)


def inner_kernel(
    strength_ref, source_ref, receiver_ref, trace_ref, along_z_ref, along_xy_ref, from_y_ref,
    fp_ref, ap_ref, fn_ref, an_ref, *refs,
):
    faces, out_ref = refs[:-1], refs[-1]
    cells_x, cells_y, cells_z = fn_ref.shape
    cells = cells_x * cells_y
    along_z = (along_z_ref[0], along_z_ref[1])
    along_xy = (along_xy_ref[0], along_xy_ref[1])
    for field, (prev_ref, now_ref) in enumerate(((fp_ref, fn_ref), (ap_ref, an_ref))):
        now = now_ref[...].reshape(cells, cells_z)
        parts = halves(now)
        total = product(parts, along_z) + product(along_xy, parts)
        total = total + (3.0 * STENCIL_WEIGHTS[0]) * now
        for side, ref in enumerate(faces):
            face = ref[field].astype(F32).reshape(cells // 2, cells_z).astype(BF16)
            for part in range(2):
                total = total + jnp.dot(from_y_ref[2 * side + part], face, preferred_element_type=F32)
        out_ref[2 + field] = total.reshape(cells_x, cells_y, cells_z)
        out_ref[field] = 2.0 * now_ref[...] - prev_ref[...]

    start_x = lax.axis_index("tx") * cells_x
    start_y = lax.axis_index("ty") * cells_y
    near_x = receiver_ref[0:1, :] - start_x
    near_y = receiver_ref[1:2, :] - start_y
    cell_x = lax.broadcasted_iota(jnp.int32, (cells_x, cells_y, near_x.shape[1]), 0)
    cell_y = lax.broadcasted_iota(jnp.int32, cell_x.shape, 1)
    hit = jnp.where((cell_x == near_x[None]) & (cell_y == near_y[None]), trace_ref[...][None], 0.0)
    surface = jnp.sum(hit, axis=2, keepdims=True)
    lanes = min(cells_z, 128)
    depth = lax.broadcasted_iota(jnp.int32, (cells_x, cells_y, lanes), 2) == SURFACE_DEPTH
    out_ref[3, :, :, :lanes] = out_ref[3, :, :, :lanes] + jnp.where(depth, surface, 0.0)
    source_x = source_ref[0, 0] - start_x
    source_y = source_ref[0, 1] - start_y

    @pl.when((source_x >= 0) & (source_x < cells_x))
    def _():
        sub = lax.broadcasted_iota(jnp.int32, (cells_y, cells_z), 0)
        lane = lax.broadcasted_iota(jnp.int32, (cells_y, cells_z), 1)
        mark = (sub == source_y) & (lane == SURFACE_DEPTH)
        out_ref[2, source_x] = out_ref[2, source_x] + jnp.where(mark, strength_ref[...], 0.0)


def edge_kernel(_, x_even_ref, x_odd_ref, state_ref):
    cells_x = state_ref.shape[1]
    at_even = lax.axis_index("tx") % 2 == 0
    for field in range(2):
        x_even = x_even_ref[field].astype(F32)
        x_odd = jnp.where(has_odd("tx"), x_odd_ref[field].astype(F32), 0.0)
        before_x = jnp.where(at_even, x_odd, x_even)
        after_x = jnp.where(at_even, x_even, x_odd)
        for place in range(REACH):
            low = state_ref[2 + field, place]
            high = state_ref[2 + field, cells_x - REACH + place]
            for layer in range(REACH):
                if place + REACH - layer <= REACH:
                    low = low + STENCIL_WEIGHTS[place + REACH - layer] * before_x[layer]
                if layer + REACH - place <= REACH:
                    high = high + STENCIL_WEIGHTS[layer + REACH - place] * after_x[layer]
            state_ref[2 + field, place] = low
            state_ref[2 + field, cells_x - REACH + place] = high


def scale_code(largest):
    least = jnp.maximum(largest, 2.0**-78) * (1.0 / 32752.0)
    exponent = jnp.floor(jnp.log2(least) + 1e-4)
    mantissa = jnp.ceil(least * jnp.exp2(7.0 - exponent))
    code = (exponent.astype(jnp.int32) + 30) * 512 + mantissa.astype(jnp.int32)
    return mantissa * jnp.exp2(exponent - 7.0), code


def scale_of(code):
    exponent = (code >> 9) - 37
    return (code & 511).astype(F32) * jnp.exp2(exponent.astype(F32))


def next_row(slot, rows_ref, blocks_ref, state_ref, slab_ref):
    r, block = rows_ref[slot], blocks_ref[slot]
    scaled = slab_ref[block].astype(F32) * STEP_RATIO
    courant = scaled * scaled
    f_next = state_ref[0, r] + courant * state_ref[2, r]
    a_next = state_ref[1, r] + courant * state_ref[3, r]
    return r, block, f_next, a_next


def send_kernel(k, rows_ref, blocks_ref, state_ref, slab_ref, message_ref, f_ref, a_ref):
    capacity, cells_y, cells_z = f_ref.shape
    lanes = message_ref.shape[1]
    parts = cells_z // lanes
    count = capacity * cells_y
    owner = lax.axis_index("shot") ^ k
    lane = lax.broadcasted_iota(jnp.int32, (cells_y, lanes), 1) // cells_y
    place = jnp.zeros((cells_y, lanes), jnp.int32)
    scales = jnp.zeros((cells_y, lanes), jnp.int32)
    images = []
    for j in range(capacity):
        _, block, f_next, a_next = next_row(owner * capacity + j, rows_ref, blocks_ref, state_ref, slab_ref)
        f_ref[j] = f_next
        a_ref[j] = a_next
        images.append(f_next * a_next)
        place = jnp.where(lane == j, block, place)
    image = jnp.concatenate(images, axis=0)
    scale, code = scale_code(jnp.max(jnp.abs(image), axis=1, keepdims=True))
    image = jnp.round(image * (1.0 / scale)).astype(jnp.int32)
    for j in range(capacity):
        scales = jnp.where(lane == j, code[j * cells_y : (j + 1) * cells_y], scales)
    for part in range(parts):
        columns = image[:, part * lanes : (part + 1) * lanes]
        message_ref[part * count : (part + 1) * count, :] = columns.astype(jnp.int16)
    message_ref[parts * count :, :] = jnp.concatenate([scales, place], axis=0).astype(jnp.int16)


def output_kernel(owners, rows_ref, blocks_ref, state_ref, slab_ref, *refs):
    others, (f_out_ref, a_out_ref, image_ref, place_ref) = refs[:-4], refs[-4:]
    cells_x, cells_y, cells_z = f_out_ref.shape
    capacity = cells_x // owners
    me = lax.axis_index("shot")
    lane = lax.broadcasted_iota(jnp.int32, place_ref.shape, 1) // cells_y
    place = jnp.zeros(place_ref.shape, jnp.int32)
    for j in range(capacity):
        r, block, f_next, a_next = next_row(me * capacity + j, rows_ref, blocks_ref, state_ref, slab_ref)
        f_out_ref[r] = f_next
        a_out_ref[r] = a_next
        image_ref[j] = f_next * a_next
        place = jnp.where(lane == j, block, place)
    place_ref[...] = place
    for n, k in enumerate(range(1, owners)):
        for j in range(capacity):
            r = rows_ref[(me ^ k) * capacity + j]
            f_out_ref[r] = others[2 * n][j]
            a_out_ref[r] = others[2 * n + 1][j]


def chosen_matrix(scales, places, slab, cells_y):
    shape = (slab,) + places.shape
    block = lax.broadcasted_iota(jnp.int32, shape, 0)
    y = lax.broadcasted_iota(jnp.int32, shape, 1)
    y_of_row = lax.broadcasted_iota(jnp.int32, shape, 2) % cells_y
    chosen = jnp.where((block == places[None]) & (y == y_of_row), scales[None], 0.0)
    return chosen.reshape(slab * cells_y, places.shape[1]).astype(BF16)


def message_parts(ref, count, cells_y, cells_z):
    lanes = ref.shape[1]
    parts = cells_z // lanes
    tail = ref[parts * count :, :count].astype(jnp.int32)
    columns = [ref[part * count : (part + 1) * count, :] for part in range(parts)]
    return scale_of(tail[:cells_y]), tail[cells_y:], jnp.concatenate(columns, axis=1).astype(F32)


def first_image_kernel(own_ref, own_place_ref, *refs):
    messages, out_ref = refs[:-1], refs[-1]
    slab, cells_y, cells_z = out_ref.shape
    count = own_ref.shape[0] * cells_y
    own = own_ref[...].reshape(count, cells_z)
    parts = [(jnp.ones((cells_y, count), F32), own_place_ref[:, :count], own)]
    parts += [message_parts(ref, count, cells_y, cells_z) for ref in messages]
    scales, places, rows = zip(*parts)
    chosen = chosen_matrix(jnp.concatenate(scales, axis=1), jnp.concatenate(places, axis=1), slab, cells_y)
    high, low = halves(jnp.concatenate(rows, axis=0))
    total = jnp.dot(chosen, high, preferred_element_type=F32) + jnp.dot(chosen, low, preferred_element_type=F32)
    out_ref[...] = total.reshape(slab, cells_y, cells_z)


def last_image_kernel(count, in_ref, message_ref, out_hbm, out_ref, sems):
    slab, cells_y, cells_z = in_ref.shape
    scales, places, rows = message_parts(message_ref, count, cells_y, cells_z)
    chosen = chosen_matrix(scales, places, slab, cells_y)
    high, low = halves(rows)
    half = slab // 2
    copies = []
    for n in range(2):
        some = chosen[n * half * cells_y : (n + 1) * half * cells_y]
        total = jnp.dot(some, high, preferred_element_type=F32) + jnp.dot(some, low, preferred_element_type=F32)
        blocks = pl.ds(n * half, half)
        out_ref[blocks] = in_ref[blocks] + total.reshape(half, cells_y, cells_z)
        copies.append(pltpu.make_async_copy(out_ref.at[blocks], out_hbm.at[blocks], sems.at[n]))
        copies[n].start()
    for copy in copies:
        copy.wait()


def in_vmem(value):
    return pltpu.with_memory_space_constraint(value, pltpu.VMEM)


def in_hbm(value):
    return pltpu.with_memory_space_constraint(value, pltpu.HBM)


def in_smem(value):
    return pltpu.with_memory_space_constraint(value, pltpu.SMEM)


def on_device(
    forward_prev,
    forward_now,
    adjoint_prev,
    adjoint_now,
    velocity_model,
    aperture,
    source_cell,
    source_strength,
    receiver_cell,
    receiver_trace,
):
    owners = lax.axis_size("shot")
    count_y = lax.axis_size("ty")
    cells_x, cells_y, cells_z = forward_now.shape[1:]
    slab = velocity_model.shape[1]
    capacity = cells_x // owners

    def peer(value, k):
        return lax.ppermute(value, "shot", [(i, i ^ k) for i in range(owners)])

    others = list(range(1, owners))
    slabs = {k: peer(velocity_model[0], k) for k in others}

    sides = 2 if count_y > 2 else 1
    field = pltpu.VMEM((cells_x, cells_y, cells_z), F32)
    x_face = pltpu.VMEM((2, REACH, cells_y, cells_z), BF16)
    y_face = pltpu.VMEM((2, cells_x // 2, cells_y, cells_z), BF16)
    table = pltpu.SMEM((cells_x,), jnp.int32)
    sources = [forward_now[0], adjoint_now[0], velocity_model[0]]
    sources += [source_cell, receiver_cell[0].T, receiver_trace, aperture]
    forward_now, adjoint_now, own_slab, source, receiver, trace, along_z, along_xy, from_y, rows, blocks, *faces = (
        pl.pallas_call(
        functools.partial(load_kernel, owners, slab),
        out_shape=(
            field,
            field,
            pltpu.VMEM(velocity_model.shape[1:], BF16),
            pltpu.SMEM(source_cell.shape, jnp.int32),
            pltpu.VMEM(sources[4].shape, jnp.int32),
            pltpu.VMEM(receiver_trace.shape, F32),
            pltpu.VMEM((2, cells_z, cells_z), BF16),
            pltpu.VMEM((2, cells_x * cells_y, cells_x * cells_y), BF16),
            pltpu.VMEM((2 * sides, cells_x * cells_y, cells_x // 2 * cells_y), BF16),
            table,
            table,
        )
        + (y_face,) * sides,
        in_specs=[HBM] * 7,
        out_specs=(VMEM,) * 3 + (SMEM,) + (VMEM,) * 5 + (SMEM,) * 2 + (VMEM,) * sides,
        scratch_shapes=[
            pltpu.SMEM(aperture.shape, jnp.int32),
            pltpu.SemaphoreType.DMA((7,)),
        ],
        compiler_params=PARAMS,
        cost_estimate=CHEAP,
        name="load_fields",
    )(*[in_hbm(value) for value in sources])
    )
    forward_now, adjoint_now = in_vmem(forward_now), in_vmem(adjoint_now)
    rows, blocks = in_smem(rows), in_smem(blocks)
    slabs[0] = own_slab
    y_halos = [in_vmem(lax.ppermute(face, ("tx", "ty"), pairs)) for face, pairs in zip(faces, swaps("ty", "tx"))]
    faces = pl.pallas_call(
        face_kernel,
        out_shape=(x_face, x_face),
        in_specs=[VMEM] * 2,
        out_specs=(VMEM, VMEM),
        compiler_params=PARAMS,
        cost_estimate=HEAVY,
        name="faces_along_x",
    )(forward_now, adjoint_now)
    odd_face = pl.pallas_call(
        after_kernel,
        out_shape=x_face,
        in_specs=[VMEM] * 2,
        out_specs=VMEM,
        compiler_params=PARAMS,
        cost_estimate=CHEAP,
        name="odd_face_after_y",
    )(in_vmem(faces[1]), y_halos[0])
    x_even, x_odd = swaps("tx", "ty")
    from_odd = lax.ppermute(odd_face, ("tx", "ty"), x_odd)
    from_even = lax.ppermute(faces[0], ("tx", "ty"), x_even)

    state = pl.pallas_call(
        inner_kernel,
        out_shape=pltpu.VMEM((4, cells_x, cells_y, cells_z), F32),
        in_specs=[VMEM, SMEM] + [VMEM] * (9 + sides),
        out_specs=VMEM,
        compiler_params=PARAMS,
        cost_estimate=LONG,
        name="inner_cells",
    )(
        source_strength[None],
        in_smem(source),
        in_vmem(receiver),
        in_vmem(trace),
        in_vmem(along_z),
        in_vmem(along_xy),
        in_vmem(from_y),
        forward_prev[0],
        adjoint_prev[0],
        forward_now,
        adjoint_now,
        *y_halos,
    )
    state = in_vmem(
        pl.pallas_call(
            edge_kernel,
            out_shape=pltpu.VMEM(state.shape, F32),
            in_specs=[VMEM] * 3,
            out_specs=VMEM,
            input_output_aliases={0: 0},
            compiler_params=PARAMS,
            cost_estimate=CHEAP,
            name="edge_cells",
        )(in_vmem(state), in_vmem(from_even), in_vmem(from_odd))
    )

    lanes = min(cells_z, 128)
    message = pltpu.VMEM(((cells_z // lanes) * capacity * cells_y + 2 * cells_y, lanes), jnp.int16)
    some_rows = pltpu.VMEM((capacity, cells_y, cells_z), F32)
    arrived, rows_of_others = [], []
    for k in others:
        rows_out, *fields = pl.pallas_call(
            functools.partial(send_kernel, k),
            out_shape=(message, some_rows, some_rows),
            in_specs=[SMEM] * 2 + [VMEM] * 2,
            out_specs=(VMEM,) * 3,
            compiler_params=PARAMS,
            cost_estimate=HEAVY if k == others[-2] else CHEAP,
            name="rows_to_send",
        )(rows, blocks, state, in_vmem(slabs[k]))
        arrived.append(peer(rows_out, k))
        rows_of_others += fields

    whole = jax.ShapeDtypeStruct((cells_x, cells_y, cells_z), F32)
    forward_next, adjoint_next, own_image, own_place = pl.pallas_call(
        functools.partial(output_kernel, owners),
        out_shape=(whole, whole, some_rows, pltpu.VMEM((cells_y, lanes), jnp.int32)),
        in_specs=[SMEM] * 2 + [VMEM] * (2 + len(rows_of_others)),
        out_specs=(VMEM,) * 4,
        compiler_params=PARAMS,
        cost_estimate=LONG,
        name="next_fields",
    )(rows, blocks, state, in_vmem(slabs[0]), *[in_vmem(other) for other in rows_of_others])

    arrived = [in_vmem(value) for value in arrived]
    image_shape = (slab, cells_y, cells_z)
    image = pl.pallas_call(
        first_image_kernel,
        out_shape=pltpu.VMEM(image_shape, F32),
        in_specs=[VMEM] * owners,
        out_specs=VMEM,
        compiler_params=PARAMS,
        cost_estimate=CHEAP,
        name="image_of_first",
    )(in_vmem(own_image), in_vmem(own_place), *arrived[1:])
    image = pl.pallas_call(
        functools.partial(last_image_kernel, capacity * cells_y),
        out_shape=jax.ShapeDtypeStruct(image_shape, F32),
        in_specs=[VMEM] * 2,
        out_specs=HBM,
        scratch_shapes=[pltpu.VMEM(image_shape, F32), pltpu.SemaphoreType.DMA((2,))],
        compiler_params=PARAMS,
        name="image_rows",
    )(in_vmem(image), arrived[0])
    return forward_next[None], adjoint_next[None], image[None]


def solution(mesh):
    in_specs = (
        P("shot", "tx", "ty", None),
        P("shot", "tx", "ty", None),
        P("shot", "tx", "ty", None),
        P("shot", "tx", "ty", None),
        P(("tx", "ty"), "shot", None, None),
        P("shot", ("tx", "ty"), None),
        P("shot", None),
        P("shot"),
        P("shot", None, None),
        P("shot", None),
    )
    out_specs = (
        P("shot", "tx", "ty", None),
        P("shot", "tx", "ty", None),
        P(("tx", "ty"), "shot", None, None),
    )
    return jax.shard_map(
        on_device, mesh=mesh, in_specs=in_specs, out_specs=out_specs, check_vma=False
    )
```

```python
import functools

import jax
import jax.numpy as jnp
from jax import lax
from jax.experimental import pallas as pl
from jax.experimental.pallas import tpu as pltpu
from jax.sharding import PartitionSpec as P

SURFACE_DEPTH = 8


STENCIL_WEIGHTS = (-205.0 / 72.0, 8.0 / 5.0, -1.0 / 5.0, 8.0 / 315.0, -1.0 / 560.0)
STEP_RATIO = 0.1
REACH = 4

VMEM = pl.BlockSpec(memory_space=pltpu.VMEM)
SMEM = pl.BlockSpec(memory_space=pltpu.SMEM)
HBM = pl.BlockSpec(memory_space=pltpu.HBM)
CHEAP = pl.CostEstimate(flops=0, bytes_accessed=0, transcendentals=0)
LONG = pl.CostEstimate(flops=0, bytes_accessed=60000000, transcendentals=0)
HEAVY = pl.CostEstimate(flops=10**10, bytes_accessed=10**8, transcendentals=10**8)
PARAMS = pltpu.CompilerParams(vmem_limit_bytes=16 * 1024 * 1024)
F32, BF16 = jnp.float32, jnp.bfloat16


def swaps(axis, other):
    count, others = lax.axis_size(axis), lax.axis_size(other)
    even = [(i, i + 1) for i in range(0, count - 1, 2)]
    odd = [(i, i + 1) for i in range(1, count - 1, 2)]

    def rank(a, o):
        return a * others + o if axis == "tx" else o * count + a

    def ranks(pairs):
        return [(rank(a, o), rank(b, o)) for a, b in pairs for o in range(others)]

    idle = [i for i in range(count) if i not in {end for pair in odd for end in pair}]
    idle = [(rank(i, o), rank(i, o + 1)) for i in idle for o in range(0, others - 1, 2)]
    return [[way for a, b in pairs for way in ((a, b), (b, a))] for pairs in (ranks(even), ranks(odd) + idle)]


def has_odd(axis):
    at = lax.axis_index(axis)
    return jnp.where(at % 2 == 0, at > 0, at < lax.axis_size(axis) - 1)


def halves(value):
    high = value.astype(BF16)
    return high, (value - high.astype(F32)).astype(BF16)


def product(left, right):
    (a, b), (c, d) = left, right

    def dot(x, y):
        return jnp.dot(x, y, preferred_element_type=F32)

    return dot(a, c) + (dot(a, d) + dot(b, c))


def by_distance(gap, stride=1):
    weights = jnp.zeros(gap.shape, F32)
    for offset in range(1, REACH + 1):
        weights = jnp.where(gap == offset * stride, STENCIL_WEIGHTS[offset], weights)
    return weights


def load_kernel(owners, slab, f_hbm, a_hbm, v_hbm, source_hbm, receiver_hbm, trace_hbm, ids_hbm, *refs):
    results, (ids_ref, sems) = refs[:-2], refs[-2:]
    f_ref, a_ref, v_ref, source_ref, receiver_ref, trace_ref, along_z_ref, along_xy_ref = results[:8]
    from_y_ref, rows_ref, blocks_ref = results[8:11]
    faces = results[11:]
    pairs = [(ids_hbm, ids_ref), (f_hbm, f_ref), (a_hbm, a_ref), (v_hbm, v_ref)]
    pairs += [(source_hbm, source_ref), (receiver_hbm, receiver_ref), (trace_hbm, trace_ref)]
    copies = [pltpu.make_async_copy(src, dst, sems.at[n]) for n, (src, dst) in enumerate(pairs)]
    for copy in copies[1:3] + copies[:1] + copies[3:]:
        copy.start()
    cells_x, cells_y, cells_z = f_ref.shape
    cells = cells_x * cells_y
    capacity = cells_x // owners
    half = cells_x // 2
    row = lax.broadcasted_iota(jnp.int32, (cells_z, cells_z), 0)
    col = lax.broadcasted_iota(jnp.int32, (cells_z, cells_z), 1)
    along_z_ref[0], along_z_ref[1] = halves(by_distance(jnp.abs(row - col)))
    row = lax.broadcasted_iota(jnp.int32, (cells, cells), 0)
    col = lax.broadcasted_iota(jnp.int32, (cells, cells), 1)
    gap = jnp.abs(row - col)
    along_y = jnp.where(row // cells_y == col // cells_y, by_distance(gap), 0.0)
    along_xy_ref[0], along_xy_ref[1] = halves(along_y + by_distance(gap, cells_y))
    at_even = lax.axis_index("ty") % 2 == 0
    row = lax.broadcasted_iota(jnp.int32, (cells, half * cells_y), 0)
    col = lax.broadcasted_iota(jnp.int32, (cells, half * cells_y), 1)
    sub = col % cells_y
    same = row // cells_y == col // cells_y + half * (sub // REACH)
    layer, y = sub % REACH, row % cells_y
    after, before = cells_y + layer - y, y + REACH - layer
    from_y_ref[0], from_y_ref[1] = halves(by_distance(jnp.where(same, jnp.where(at_even, after, before), 0)))
    if len(faces) > 1:
        same &= has_odd("ty")
        from_y_ref[2], from_y_ref[3] = halves(by_distance(jnp.where(same, jnp.where(at_even, before, after), 0)))

    copies[0].wait()
    bits = 32 // owners
    taken = jnp.int32(0)
    for r in range(cells_x):
        block = ids_ref[0, 0, r]
        owner = block // slab
        slot = owner * capacity + ((taken >> (owner * bits)) & (2**bits - 1))
        rows_ref[slot] = r
        blocks_ref[slot] = block - owner * slab
        taken = taken + (1 << (owner * bits))
    low = (lax.broadcasted_iota(jnp.int32, (half, cells_y, cells_z), 1) < REACH).astype(jnp.int32)
    for field, ref in enumerate((f_ref, a_ref)):
        copies[1 + field].wait()
        for face, tails in zip(faces, (at_even, jnp.logical_not(at_even))):
            turn = jnp.where(tails, 0, half)
            turned = pltpu.roll(ref[pl.ds(turn, half)], REACH, 1)
            straight = ref[pl.ds(half - turn, half)]
            face[field] = jnp.where(low == tails.astype(jnp.int32), turned, straight).astype(BF16)
    for copy in copies[3:]:
        copy.wait()


def after_kernel(in_ref, _, out_ref):
    out_ref[...] = in_ref[...]


def face_kernel(f_ref, a_ref, even_ref, odd_ref):
    at_even = lax.axis_index("tx") % 2 == 0
    tail, head = f_ref.shape[0] - REACH, 0
    for field, ref in enumerate((f_ref, a_ref)):
        even_ref[field] = ref[pl.ds(jnp.where(at_even, tail, head), REACH)].astype(BF16)
        odd_ref[field] = ref[pl.ds(jnp.where(at_even, head, tail), REACH)].astype(BF16)


def inner_kernel(
    strength_ref, source_ref, receiver_ref, trace_ref, along_z_ref, along_xy_ref, from_y_ref,
    fp_ref, ap_ref, fn_ref, an_ref, *refs,
):
    faces, out_ref = refs[:-1], refs[-1]
    cells_x, cells_y, cells_z = fn_ref.shape
    cells = cells_x * cells_y
    along_z = (along_z_ref[0], along_z_ref[1])
    along_xy = (along_xy_ref[0], along_xy_ref[1])
    for field, (prev_ref, now_ref) in enumerate(((fp_ref, fn_ref), (ap_ref, an_ref))):
        now = now_ref[...].reshape(cells, cells_z)
        parts = halves(now)
        total = product(parts, along_z) + product(along_xy, parts)
        total = total + (3.0 * STENCIL_WEIGHTS[0]) * now
        for side, ref in enumerate(faces):
            face = ref[field].astype(F32).reshape(cells // 2, cells_z).astype(BF16)
            for part in range(2):
                total = total + jnp.dot(from_y_ref[2 * side + part], face, preferred_element_type=F32)
        out_ref[2 + field] = total.reshape(cells_x, cells_y, cells_z)
        out_ref[field] = 2.0 * now_ref[...] - prev_ref[...]

    start_x = lax.axis_index("tx") * cells_x
    start_y = lax.axis_index("ty") * cells_y
    near_x = receiver_ref[0:1, :] - start_x
    near_y = receiver_ref[1:2, :] - start_y
    cell_x = lax.broadcasted_iota(jnp.int32, (cells_x, cells_y, near_x.shape[1]), 0)
    cell_y = lax.broadcasted_iota(jnp.int32, cell_x.shape, 1)
    hit = jnp.where((cell_x == near_x[None]) & (cell_y == near_y[None]), trace_ref[...][None], 0.0)
    surface = jnp.sum(hit, axis=2, keepdims=True)
    lanes = min(cells_z, 128)
    depth = lax.broadcasted_iota(jnp.int32, (cells_x, cells_y, lanes), 2) == SURFACE_DEPTH
    out_ref[3, :, :, :lanes] = out_ref[3, :, :, :lanes] + jnp.where(depth, surface, 0.0)
    source_x = source_ref[0, 0] - start_x
    source_y = source_ref[0, 1] - start_y

    @pl.when((source_x >= 0) & (source_x < cells_x))
    def _():
        sub = lax.broadcasted_iota(jnp.int32, (cells_y, cells_z), 0)
        lane = lax.broadcasted_iota(jnp.int32, (cells_y, cells_z), 1)
        mark = (sub == source_y) & (lane == SURFACE_DEPTH)
        out_ref[2, source_x] = out_ref[2, source_x] + jnp.where(mark, strength_ref[...], 0.0)


def edge_kernel(_, x_even_ref, x_odd_ref, state_ref):
    cells_x = state_ref.shape[1]
    at_even = lax.axis_index("tx") % 2 == 0
    for field in range(2):
        x_even = x_even_ref[field].astype(F32)
        x_odd = jnp.where(has_odd("tx"), x_odd_ref[field].astype(F32), 0.0)
        before_x = jnp.where(at_even, x_odd, x_even)
        after_x = jnp.where(at_even, x_even, x_odd)
        for place in range(REACH):
            low = state_ref[2 + field, place]
            high = state_ref[2 + field, cells_x - REACH + place]
            for layer in range(REACH):
                if place + REACH - layer <= REACH:
                    low = low + STENCIL_WEIGHTS[place + REACH - layer] * before_x[layer]
                if layer + REACH - place <= REACH:
                    high = high + STENCIL_WEIGHTS[layer + REACH - place] * after_x[layer]
            state_ref[2 + field, place] = low
            state_ref[2 + field, cells_x - REACH + place] = high


def scale_code(largest):
    least = jnp.maximum(largest, 2.0**-78) * (1.0 / 32752.0)
    exponent = jnp.floor(jnp.log2(least) + 1e-4)
    mantissa = jnp.ceil(least * jnp.exp2(7.0 - exponent))
    code = (exponent.astype(jnp.int32) + 30) * 512 + mantissa.astype(jnp.int32)
    return mantissa * jnp.exp2(exponent - 7.0), code


def scale_of(code):
    exponent = (code >> 9) - 37
    return (code & 511).astype(F32) * jnp.exp2(exponent.astype(F32))


def next_row(slot, rows_ref, blocks_ref, state_ref, slab_ref):
    r, block = rows_ref[slot], blocks_ref[slot]
    scaled = slab_ref[block].astype(F32) * STEP_RATIO
    courant = scaled * scaled
    f_next = state_ref[0, r] + courant * state_ref[2, r]
    a_next = state_ref[1, r] + courant * state_ref[3, r]
    return r, block, f_next, a_next


def send_kernel(k, rows_ref, blocks_ref, state_ref, slab_ref, message_ref, f_ref, a_ref):
    capacity, cells_y, cells_z = f_ref.shape
    lanes = message_ref.shape[1]
    parts = cells_z // lanes
    count = capacity * cells_y
    owner = lax.axis_index("shot") ^ k
    lane = lax.broadcasted_iota(jnp.int32, (cells_y, lanes), 1) // cells_y
    place = jnp.zeros((cells_y, lanes), jnp.int32)
    scales = jnp.zeros((cells_y, lanes), jnp.int32)
    images = []
    for j in range(capacity):
        _, block, f_next, a_next = next_row(owner * capacity + j, rows_ref, blocks_ref, state_ref, slab_ref)
        f_ref[j] = f_next
        a_ref[j] = a_next
        images.append(f_next * a_next)
        place = jnp.where(lane == j, block, place)
    image = jnp.concatenate(images, axis=0)
    scale, code = scale_code(jnp.max(jnp.abs(image), axis=1, keepdims=True))
    image = jnp.round(image * (1.0 / scale)).astype(jnp.int32)
    for j in range(capacity):
        scales = jnp.where(lane == j, code[j * cells_y : (j + 1) * cells_y], scales)
    for part in range(parts):
        columns = image[:, part * lanes : (part + 1) * lanes]
        message_ref[part * count : (part + 1) * count, :] = columns.astype(jnp.int16)
    message_ref[parts * count :, :] = jnp.concatenate([scales, place], axis=0).astype(jnp.int16)


def output_kernel(owners, rows_ref, blocks_ref, state_ref, slab_ref, *refs):
    others, (f_out_ref, a_out_ref, image_ref, place_ref) = refs[:-4], refs[-4:]
    cells_x, cells_y, cells_z = f_out_ref.shape
    capacity = cells_x // owners
    me = lax.axis_index("shot")
    lane = lax.broadcasted_iota(jnp.int32, place_ref.shape, 1) // cells_y
    place = jnp.zeros(place_ref.shape, jnp.int32)
    for j in range(capacity):
        r, block, f_next, a_next = next_row(me * capacity + j, rows_ref, blocks_ref, state_ref, slab_ref)
        f_out_ref[r] = f_next
        a_out_ref[r] = a_next
        image_ref[j] = f_next * a_next
        place = jnp.where(lane == j, block, place)
    place_ref[...] = place
    for n, k in enumerate(range(1, owners)):
        for j in range(capacity):
            r = rows_ref[(me ^ k) * capacity + j]
            f_out_ref[r] = others[2 * n][j]
            a_out_ref[r] = others[2 * n + 1][j]


def chosen_matrix(scales, places, slab, cells_y):
    shape = (slab,) + places.shape
    block = lax.broadcasted_iota(jnp.int32, shape, 0)
    y = lax.broadcasted_iota(jnp.int32, shape, 1)
    y_of_row = lax.broadcasted_iota(jnp.int32, shape, 2) % cells_y
    chosen = jnp.where((block == places[None]) & (y == y_of_row), scales[None], 0.0)
    return chosen.reshape(slab * cells_y, places.shape[1]).astype(BF16)


def message_parts(ref, count, cells_y, cells_z):
    lanes = ref.shape[1]
    parts = cells_z // lanes
    tail = ref[parts * count :, :count].astype(jnp.int32)
    columns = [ref[part * count : (part + 1) * count, :] for part in range(parts)]
    return scale_of(tail[:cells_y]), tail[cells_y:], jnp.concatenate(columns, axis=1).astype(F32)


def first_image_kernel(own_ref, own_place_ref, *refs):
    messages, out_ref = refs[:-1], refs[-1]
    slab, cells_y, cells_z = out_ref.shape
    count = own_ref.shape[0] * cells_y
    own = own_ref[...].reshape(count, cells_z)
    parts = [(jnp.ones((cells_y, count), F32), own_place_ref[:, :count], own)]
    parts += [message_parts(ref, count, cells_y, cells_z) for ref in messages]
    scales, places, rows = zip(*parts)
    chosen = chosen_matrix(jnp.concatenate(scales, axis=1), jnp.concatenate(places, axis=1), slab, cells_y)
    high, low = halves(jnp.concatenate(rows, axis=0))
    total = jnp.dot(chosen, high, preferred_element_type=F32) + jnp.dot(chosen, low, preferred_element_type=F32)
    out_ref[...] = total.reshape(slab, cells_y, cells_z)


def last_image_kernel(count, in_ref, message_ref, out_hbm, out_ref, sems):
    slab, cells_y, cells_z = in_ref.shape
    scales, places, rows = message_parts(message_ref, count, cells_y, cells_z)
    chosen = chosen_matrix(scales, places, slab, cells_y)
    high, low = halves(rows)
    half = slab // 2
    copies = []
    for n in range(2):
        some = chosen[n * half * cells_y : (n + 1) * half * cells_y]
        total = jnp.dot(some, high, preferred_element_type=F32) + jnp.dot(some, low, preferred_element_type=F32)
        blocks = pl.ds(n * half, half)
        out_ref[blocks] = in_ref[blocks] + total.reshape(half, cells_y, cells_z)
        copies.append(pltpu.make_async_copy(out_ref.at[blocks], out_hbm.at[blocks], sems.at[n]))
        copies[n].start()
    for copy in copies:
        copy.wait()


def in_vmem(value):
    return pltpu.with_memory_space_constraint(value, pltpu.VMEM)


def in_hbm(value):
    return pltpu.with_memory_space_constraint(value, pltpu.HBM)


def in_smem(value):
    return pltpu.with_memory_space_constraint(value, pltpu.SMEM)


def on_device(
    forward_prev,
    forward_now,
    adjoint_prev,
    adjoint_now,
    velocity_model,
    aperture,
    source_cell,
    source_strength,
    receiver_cell,
    receiver_trace,
):
    owners = lax.axis_size("shot")
    count_y = lax.axis_size("ty")
    cells_x, cells_y, cells_z = forward_now.shape[1:]
    slab = velocity_model.shape[1]
    capacity = cells_x // owners

    def peer(value, k):
        return lax.ppermute(value, "shot", [(i, i ^ k) for i in range(owners)])

    others = list(range(1, owners))
    slabs = {k: peer(velocity_model[0], k) for k in others}

    sides = 2 if count_y > 2 else 1
    field = pltpu.VMEM((cells_x, cells_y, cells_z), F32)
    x_face = pltpu.VMEM((2, REACH, cells_y, cells_z), BF16)
    y_face = pltpu.VMEM((2, cells_x // 2, cells_y, cells_z), BF16)
    table = pltpu.SMEM((cells_x,), jnp.int32)
    sources = [forward_now[0], adjoint_now[0], velocity_model[0]]
    sources += [source_cell, receiver_cell[0].T, receiver_trace, aperture]
    forward_now, adjoint_now, own_slab, source, receiver, trace, along_z, along_xy, from_y, rows, blocks, *faces = (
        pl.pallas_call(
        functools.partial(load_kernel, owners, slab),
        out_shape=(
            field,
            field,
            pltpu.VMEM(velocity_model.shape[1:], BF16),
            pltpu.SMEM(source_cell.shape, jnp.int32),
            pltpu.VMEM(sources[4].shape, jnp.int32),
            pltpu.VMEM(receiver_trace.shape, F32),
            pltpu.VMEM((2, cells_z, cells_z), BF16),
            pltpu.VMEM((2, cells_x * cells_y, cells_x * cells_y), BF16),
            pltpu.VMEM((2 * sides, cells_x * cells_y, cells_x // 2 * cells_y), BF16),
            table,
            table,
        )
        + (y_face,) * sides,
        in_specs=[HBM] * 7,
        out_specs=(VMEM,) * 3 + (SMEM,) + (VMEM,) * 5 + (SMEM,) * 2 + (VMEM,) * sides,
        scratch_shapes=[
            pltpu.SMEM(aperture.shape, jnp.int32),
            pltpu.SemaphoreType.DMA((7,)),
        ],
        compiler_params=PARAMS,
        cost_estimate=CHEAP,
        name="load_fields",
    )(*[in_hbm(value) for value in sources])
    )
    forward_now, adjoint_now = in_vmem(forward_now), in_vmem(adjoint_now)
    rows, blocks = in_smem(rows), in_smem(blocks)
    slabs[0] = own_slab
    y_halos = [in_vmem(lax.ppermute(face, ("tx", "ty"), pairs)) for face, pairs in zip(faces, swaps("ty", "tx"))]
    faces = pl.pallas_call(
        face_kernel,
        out_shape=(x_face, x_face),
        in_specs=[VMEM] * 2,
        out_specs=(VMEM, VMEM),
        compiler_params=PARAMS,
        cost_estimate=HEAVY,
        name="faces_along_x",
    )(forward_now, adjoint_now)
    odd_face = pl.pallas_call(
        after_kernel,
        out_shape=x_face,
        in_specs=[VMEM] * 2,
        out_specs=VMEM,
        compiler_params=PARAMS,
        cost_estimate=CHEAP,
        name="odd_face_after_y",
    )(in_vmem(faces[1]), y_halos[0])
    x_even, x_odd = swaps("tx", "ty")
    from_odd = lax.ppermute(odd_face, ("tx", "ty"), x_odd)
    from_even = lax.ppermute(faces[0], ("tx", "ty"), x_even)

    state = pl.pallas_call(
        inner_kernel,
        out_shape=pltpu.VMEM((4, cells_x, cells_y, cells_z), F32),
        in_specs=[VMEM, SMEM] + [VMEM] * (9 + sides),
        out_specs=VMEM,
        compiler_params=PARAMS,
        cost_estimate=LONG,
        name="inner_cells",
    )(
        source_strength[None],
        in_smem(source),
        in_vmem(receiver),
        in_vmem(trace),
        in_vmem(along_z),
        in_vmem(along_xy),
        in_vmem(from_y),
        forward_prev[0],
        adjoint_prev[0],
        forward_now,
        adjoint_now,
        *y_halos,
    )
    state = in_vmem(
        pl.pallas_call(
            edge_kernel,
            out_shape=pltpu.VMEM(state.shape, F32),
            in_specs=[VMEM] * 3,
            out_specs=VMEM,
            input_output_aliases={0: 0},
            compiler_params=PARAMS,
            cost_estimate=CHEAP,
            name="edge_cells",
        )(in_vmem(state), in_vmem(from_even), in_vmem(from_odd))
    )

    lanes = min(cells_z, 128)
    message = pltpu.VMEM(((cells_z // lanes) * capacity * cells_y + 2 * cells_y, lanes), jnp.int16)
    some_rows = pltpu.VMEM((capacity, cells_y, cells_z), F32)
    arrived, rows_of_others = [], []
    for k in others:
        rows_out, *fields = pl.pallas_call(
            functools.partial(send_kernel, k),
            out_shape=(message, some_rows, some_rows),
            in_specs=[SMEM] * 2 + [VMEM] * 2,
            out_specs=(VMEM,) * 3,
            compiler_params=PARAMS,
            cost_estimate=HEAVY if k == others[-2] else CHEAP,
            name="rows_to_send",
        )(rows, blocks, state, in_vmem(slabs[k]))
        arrived.append(peer(rows_out, k))
        rows_of_others += fields

    whole = jax.ShapeDtypeStruct((cells_x, cells_y, cells_z), F32)
    forward_next, adjoint_next, own_image, own_place = pl.pallas_call(
        functools.partial(output_kernel, owners),
        out_shape=(whole, whole, some_rows, pltpu.VMEM((cells_y, lanes), jnp.int32)),
        in_specs=[SMEM] * 2 + [VMEM] * (2 + len(rows_of_others)),
        out_specs=(VMEM,) * 4,
        compiler_params=PARAMS,
        cost_estimate=LONG,
        name="next_fields",
    )(rows, blocks, state, in_vmem(slabs[0]), *[in_vmem(other) for other in rows_of_others])

    arrived = [in_vmem(value) for value in arrived]
    image_shape = (slab, cells_y, cells_z)
    image = pl.pallas_call(
        first_image_kernel,
        out_shape=pltpu.VMEM(image_shape, F32),
        in_specs=[VMEM] * owners,
        out_specs=VMEM,
        compiler_params=PARAMS,
        cost_estimate=CHEAP,
        name="image_of_first",
    )(in_vmem(own_image), in_vmem(own_place), *arrived[1:])
    image = pl.pallas_call(
        functools.partial(last_image_kernel, capacity * cells_y),
        out_shape=jax.ShapeDtypeStruct(image_shape, F32),
        in_specs=[VMEM] * 2,
        out_specs=HBM,
        scratch_shapes=[pltpu.VMEM(image_shape, F32), pltpu.SemaphoreType.DMA((2,))],
        compiler_params=PARAMS,
        name="image_rows",
    )(in_vmem(image), arrived[0])
    return forward_next[None], adjoint_next[None], image[None]


def solution(mesh):
    in_specs = (
        P("shot", "tx", "ty", None),
        P("shot", "tx", "ty", None),
        P("shot", "tx", "ty", None),
        P("shot", "tx", "ty", None),
        P(("tx", "ty"), "shot", None, None),
        P("shot", ("tx", "ty"), None),
        P("shot", None),
        P("shot"),
        P("shot", None, None),
        P("shot", None),
    )
    out_specs = (
        P("shot", "tx", "ty", None),
        P("shot", "tx", "ty", None),
        P(("tx", "ty"), "shot", None, None),
    )
    return jax.shard_map(
        on_device, mesh=mesh, in_specs=in_specs, out_specs=out_specs, check_vma=False
    )
```
